32 devices in a mesh: seq: 8 (over y, x, core), head: 4 (over z).
Axes of the slice: x: 2, y: 2, z: 4, core: 2. Of those that a mesh axis runs over, the one named last changes fastest.
Arguments:
- layer_input: bfloat16 [16384, 768], P('seq'), may hold values from -6 to 6
- gain_in: float32 [768], replicated, may hold values from 0.5 to 1.5
- w_gate: bfloat16 [768, 1536], P(None, 'head'), may hold values from -0.21875 to 0.21875
- w_inner: bfloat16 [768, 1536], P(None, 'head'), may hold values from -0.21875 to 0.21875
- w_bc: bfloat16 [768, 256], replicated, may hold values from -0.21875 to 0.21875
- w_step: bfloat16 [768, 24], P(None, 'head'), may hold values from -0.21875 to 0.21875
- conv_inner: float32 [4, 1536], P(None, 'head'), may hold values from -3 to 3
- conv_inner_bias: float32 [1536], P('head'), may hold values from -1.5 to 1.5
- conv_bc: float32 [4, 256], replicated, may hold values from -3 to 3
- conv_bc_bias: float32 [256], replicated, may hold values from -1.5 to 1.5
- step_bias: float32 [24], P('head'), may hold values from -2 to 0.5
- decay_log: float32 [24], P('head')
- skip_gain: float32 [24], P('head'), may hold values from 0.5 to 1.5
- gain_out: float32 [1536], P('head'), may hold values from 0.5 to 1.5
- w_out: bfloat16 [1536, 768], P('head'), may hold values from -0.15625 to 0.15625
- output_grad: bfloat16 [16384, 768], P('seq', 'head'), may hold values from -6 to 6
Outputs:
- mixed: bfloat16 [16384, 768], P('seq', 'head')
- grad_input: float32 [16384, 768], P('seq')
- grad_gain_in: float32 [768], replicated
- grad_w_gate: float32 [768, 1536], P(None, 'head')
- grad_w_inner: float32 [768, 1536], P(None, 'head')
- grad_w_bc: float32 [768, 256], replicated
- grad_w_step: float32 [768, 24], P(None, 'head')
- grad_conv_inner: float32 [4, 1536], P(None, 'head')
- grad_conv_inner_bias: float32 [1536], P('head')
- grad_conv_bc: float32 [4, 256], replicated
- grad_conv_bc_bias: float32 [256], replicated
- grad_step_bias: float32 [24], P('head')
- grad_decay_log: float32 [24], P('head')
- grad_skip_gain: float32 [24], P('head')
- grad_gain_out: float32 [1536], P('head')
- grad_w_out: float32 [1536, 768], P('head')
The draws below stay inside these ranges and needn't reach their ends.
All inputs are finite; a program needn't handle non-finite values.
Results may differ from the reference program's by a relative error of at most 0.012.
The reference program's roundings to bfloat16 on the way count: a program that leaves them out, or rounds other values in their place, can miss the bound.
Values may be sent and summed in bfloat16 or wider, within the bound.
No kernel may reach another device: no remote copies, remote signals or barrier semaphores. Data moves between devices by JAX's collectives and lax.ppermute only.
A program may use at most 192 MiB of HBM per device.

```python
import math
import jax
import jax.numpy as jnp
from jax import lax

D = 768
HEADS = 24
HDIM = 64
NSTATE = 128
KERNEL = 4
GROUP = 256
DI = 1536
LENGTH = 16384


def draw_decay_log(key, part):
    key = jax.random.fold_in(key, 11)
    spread = jax.random.uniform(key, (HEADS,), jnp.float32)
    low_end = math.log(0.5 / LENGTH)
    high_end = math.log(0.05)
    return low_end + (high_end - low_end) * spread


def shard_levels(key, dims, cuts, smallest, high):
    loudness, own = 1.0, jax.random.fold_in(key, 6)
    for position, parts in cuts:
        steps = jnp.exp(jax.random.uniform(jax.random.fold_in(own, position), (parts,), jnp.float32, smallest / len(cuts), high / len(cuts)))
        loudness = loudness * jnp.repeat(steps, dims[position] // parts).reshape([-1 if axis == position else 1 for axis in range(len(dims))])
    return loudness


def bell_draw(key, shape, deviation, limit, cuts=(), kind=jnp.bfloat16):
    values = jax.random.normal(key, shape, jnp.float32) * deviation
    if len(cuts) > 0:
        values = shard_levels(key, shape, cuts, -0.22, 0.18) * values
    return jnp.clip(values, min=-limit, max=limit).astype(kind)


def setup_inputs(seed: int = 0) -> dict:
    streams_of = jax.random.split(jax.random.key(seed), 17)
    layer_input = bell_draw(streams_of[0], (LENGTH, D), 1.0, 6.0, ((0, 8),))
    gain_in = jnp.clip(1.0 + 0.1 * jax.random.normal(streams_of[1], (D,), jnp.float32), 0.5, 1.5)
    w_gate = bell_draw(streams_of[2], (D, DI), D ** -0.5, 0.21875, ((1, 4),))
    w_inner = bell_draw(streams_of[3], (D, DI), D ** -0.5, 0.21875, ((1, 4),))
    w_bc = bell_draw(streams_of[4], (D, 2 * NSTATE), D ** -0.5, 0.21875)
    w_step = bell_draw(streams_of[5], (D, HEADS), D ** -0.5, 0.21875, ((1, 4),))
    conv_inner = bell_draw(streams_of[6], (KERNEL, DI), 0.5, 3.0, ((1, 4),), jnp.float32)
    conv_inner_bias = bell_draw(streams_of[7], (DI,), 0.3, 1.5, ((0, 4),), jnp.float32)
    conv_bc = bell_draw(streams_of[8], (KERNEL, 2 * NSTATE), 0.5, 3.0, (), jnp.float32)
    conv_bc_bias = bell_draw(streams_of[9], (2 * NSTATE,), 0.3, 1.5, (), jnp.float32)
    step_bias = jnp.clip(-2.0 + 2.5 * jax.random.uniform(streams_of[10], (HEADS,), jnp.float32) ** shard_levels(streams_of[10], (HEADS,), ((0, 4),), -0.2, 0.2), -2.0, 0.5)
    decay_log = draw_decay_log(jax.random.fold_in(streams_of[16], 71), 0)
    skip_gain = jnp.clip(0.5 + 1.0 * jax.random.uniform(streams_of[12], (HEADS,), jnp.float32) ** shard_levels(streams_of[12], (HEADS,), ((0, 4),), -0.2, 0.2), 0.5, 1.5)
    gain_out = jnp.clip(1.0 + 0.1 * jax.random.normal(streams_of[13], (DI,), jnp.float32), 0.5, 1.5)
    w_out = bell_draw(streams_of[14], (DI, D), DI ** -0.5, 0.15625, ((0, 4),))
    output_grad = bell_draw(streams_of[15], (LENGTH, D), 1.0, 6.0, ((0, 8), (1, 4)))
    return dict(layer_input=layer_input, gain_in=gain_in, w_gate=w_gate, w_inner=w_inner, w_bc=w_bc, w_step=w_step, conv_inner=conv_inner, conv_inner_bias=conv_inner_bias, conv_bc=conv_bc, conv_bc_bias=conv_bc_bias, step_bias=step_bias, decay_log=decay_log, skip_gain=skip_gain, gain_out=gain_out, w_out=w_out, output_grad=output_grad)


HIGH = lax.Precision.HIGHEST
eps = 1e-05

@jax.custom_vjp
def low(v):
    return lax.optimization_barrier(v.astype(jnp.bfloat16)).astype(jnp.float32)

@jax.custom_vjp
def low_back(v):
    return v

def low_keep(v):
    return (low(v), None)

def low_pass(kept, grad):
    return (grad,)

def back_keep(v):
    return (v, None)

def back_low(kept, grad):
    return (low(grad),)
low.defvjp(low_keep, low_pass)
low_back.defvjp(back_keep, back_low)

def causal_conv(values, weights, bias):
    count = values.shape[0]
    padded = jnp.concatenate([jnp.zeros((KERNEL - 1, values.shape[1]), values.dtype), values], 0)
    total = bias[None, :] + sum((weights[tap][None, :] * padded[tap:tap + count] for tap in range(KERNEL)))
    return jax.nn.silu(total)

def group_step(state, pieces):
    inner, keys, queries, step, rate = pieces
    cum = jnp.cumsum(rate, axis=0)
    scores = jnp.dot(queries, keys.T, precision=HIGH)
    lower = (jnp.arange(GROUP)[:, None] >= jnp.arange(GROUP)[None, :])[:, :, None]
    diff = cum[:, None, :] - cum[None, :, :]
    decay = jnp.where(lower, jnp.exp(jnp.where(lower, diff, 0.0)), 0.0)
    mixing = scores[:, :, None] * decay * step[None, :, :]
    output = jnp.einsum('ijh,jhp->ihp', mixing, inner, precision=HIGH)
    output = output + jnp.exp(cum)[:, :, None] * jnp.einsum('hpn,in->ihp', state, queries, precision=HIGH)
    tail = jnp.exp(cum[-1][None, :] - cum) * step
    fresh = jnp.einsum('jh,jhp,jn->hpn', tail, inner, keys, precision=HIGH)
    new_state = jnp.exp(cum[-1])[:, None, None] * state + fresh
    return (new_state, output)

def forward(layer_x, gain_in, w_gate, w_inner, w_bc, w_step, conv_inner, conv_inner_bias, conv_bc, conv_bc_bias, step_bias, decay_log, skip_gain, gain_out, w_out):
    mean_sq = lax.optimization_barrier(jnp.mean(layer_x * layer_x, -1, keepdims=True))
    normed = low(layer_x * lax.rsqrt(mean_sq + eps) * gain_in)
    gate = low_back(jnp.dot(normed, w_gate, precision=HIGH))
    inner_pre = low_back(jnp.dot(normed, w_inner, precision=HIGH))
    bc_pre = jnp.dot(normed, w_bc, precision=HIGH)
    step_raw = jnp.dot(normed, w_step, precision=HIGH)
    inner = causal_conv(inner_pre, conv_inner, conv_inner_bias)
    both = causal_conv(bc_pre, conv_bc, conv_bc_bias)
    keys = both[:, :NSTATE]
    queries = both[:, NSTATE:]
    step = jax.nn.softplus(step_raw + step_bias)
    rate = -jnp.exp(decay_log) * step
    blocks = LENGTH // GROUP
    inner3 = inner.reshape(blocks, GROUP, HEADS, HDIM)
    pieces = (inner3, keys.reshape(blocks, GROUP, NSTATE), queries.reshape(blocks, GROUP, NSTATE), step.reshape(blocks, GROUP, HEADS), rate.reshape(blocks, GROUP, HEADS))
    start = jnp.zeros((HEADS, HDIM, NSTATE), layer_x.dtype)
    final, outputs = lax.scan(jax.checkpoint(group_step), start, pieces)
    ssd = outputs + skip_gain[None, None, :, None] * inner3
    mixed_inner = ssd.reshape(LENGTH, DI) * jax.nn.silu(gate)
    out_sq = lax.optimization_barrier(jnp.mean(mixed_inner * mixed_inner, -1, keepdims=True))
    normed_out = low(mixed_inner * lax.rsqrt(out_sq + eps) * gain_out)
    return layer_x + jnp.dot(normed_out, w_out, precision=HIGH)

def reference(layer_input, gain_in, w_gate, w_inner, w_bc, w_step, conv_inner, conv_inner_bias, conv_bc, conv_bc_bias, step_bias, decay_log, skip_gain, gain_out, w_out, output_grad):
    primals = (layer_input.astype(jnp.float32), gain_in, w_gate.astype(jnp.float32), w_inner.astype(jnp.float32), w_bc.astype(jnp.float32), w_step.astype(jnp.float32), conv_inner, conv_inner_bias, conv_bc, conv_bc_bias, step_bias, decay_log, skip_gain, gain_out, w_out.astype(jnp.float32))
    result, pull = jax.vjp(forward, *primals)
    grads = pull(output_grad.astype(jnp.float32))
    return (result.astype(jnp.bfloat16), grads[0], grads[1], grads[2], grads[3], grads[4], grads[5], grads[6], grads[7], grads[8], grads[9], grads[10], grads[11], grads[12], grads[13], grads[14])
```

```python
import functools
import jax
import jax.numpy as jnp
from jax import lax
from jax.experimental import pallas as pl
from jax.experimental.pallas import tpu as pltpu
from jax.sharding import PartitionSpec as P

BLOCK = 256
LANES = 128
EDGE = 16
F32, BF16 = jnp.float32, jnp.bfloat16
eps = 1e-05


def turn(block, axis, distance):
    count = lax.axis_size(axis)
    return lax.ppermute(block, axis, [(i, (i + distance) % count) for i in range(count)])


def shifted(block, axis, distance):
    devices = range(lax.axis_size(axis))
    return lax.ppermute(block, axis, [(i - distance, i) for i in devices if i - distance in devices])


def ring_gather(block, axis):
    pieces = [block]
    for _ in range(lax.axis_size(axis) - 1):
        pieces.append(turn(pieces[-1], axis, 1))
    return pieces


def ring_scatter(parts, axis):
    count, mine = lax.axis_size(axis), lax.axis_index(axis)
    total = parts((mine - 1) % count)
    for step in range(count - 1):
        arrived = turn(total, axis, 1)
        own = parts((mine - 2 - step) % count)
        total = arrived.astype(F32) + own.astype(F32)
        if step < count - 2:
            total = total.astype(BF16)
    return total


def small_sum(value, axis):
    total = value
    for step in range(1, lax.axis_size(axis)):
        total = total + turn(value, axis, step)
    return total


def butterfly(value, axis):
    count, reach = lax.axis_size(axis), 1
    while reach < count:
        value = value + lax.ppermute(value, axis, [(i, i ^ reach) for i in range(count)])
        reach *= 2
    return value


def joined_states(payload, axis, width, heads, backward):
    count, mine = lax.axis_size(axis), lax.axis_index(axis)
    pieces = [lax.all_gather(part, axis).astype(F32) for part in payload]
    pieces = pieces[0] + pieces[1]
    logs = pieces[:, width, :heads]
    states = pieces[:, :width]
    place = jnp.arange(count)
    k, m = place[:, None], place[None, :]
    if backward:
        between, counted = (m > mine) & (m < k), place > mine
    else:
        between, counted = (m > k) & (m < mine), place < mine
    passed = jnp.sum(jnp.where(between[:, :, None], logs[None], 0.0), 1)
    weight = jnp.where(counted[:, None], jnp.exp(passed), 0.0)
    weight = jnp.repeat(weight, width // heads, 1)
    return jnp.sum(weight[:, :, None] * states, 0)


def dot(left, right, left_dim=1, right_dim=0, precision=None):
    return lax.dot_general(
        left, right, (((left_dim,), (right_dim,)), ((), ())), precision=precision, preferred_element_type=F32
    )


def silu(value):
    return value * jax.nn.sigmoid(value)


def silu_slope(value):
    s = jax.nn.sigmoid(value)
    return s * (1.0 + value * (1.0 - s))


def halves(value):
    coarse = value.astype(BF16)
    return coarse, (value - coarse.astype(F32)).astype(BF16)


def dot_left(left, right, left_dim=1, right_dim=0):
    coarse, fine = halves(left)
    return dot(coarse, right, left_dim, right_dim) + dot(fine, right, left_dim, right_dim)


def dot_right(left, right, left_dim=1, right_dim=0):
    coarse, fine = halves(right)
    return dot(left, coarse, left_dim, right_dim) + dot(left, fine, left_dim, right_dim)


def dot_both(left, right, left_dim=1, right_dim=0):
    coarse, fine = halves(left)
    return dot_right(coarse, right, left_dim, right_dim) + dot(fine, right.astype(BF16), left_dim, right_dim)


def steps(raw, step_bias):
    moved = raw + step_bias
    return moved, jnp.maximum(moved, 0.0) + jnp.log1p(jnp.exp(-jnp.abs(moved)))


def widen(value, spread):
    return dot_left(value, spread)


def narrow(value, spread):
    return dot_left(value, spread, 1, 1)


def state_decay(last, spread):
    return dot_right(spread, jnp.broadcast_to(jnp.exp(last), (LANES, LANES)).T, 0, 0)


def as_columns(rows, width):
    return dot_left(rows, jnp.full((rows.shape[0], width), 1.0 / rows.shape[0], BF16), 0, 0)


def as_rows(value):
    return dot_right(jnp.ones((8, value.shape[1]), BF16), value, 1, 1)


def row_sum(value):
    return jnp.sum(value, 0, keepdims=True)


def forward_kernel(
    x, halo, gain, w_gate, w_inner, w_bc, w_step, taps, bias, step_bias, decay_log, lower, spread,
    normed_o, gate_o, pre_o, tot_o, raw_o, cum_o, cum_rows_o, local_o, payload_o,
    before, state, passed,
):
    here, length, width = pl.program_id(0), x.shape[0], w_gate.shape[1]

    def norm(rows):
        rows = rows.astype(F32)
        return (rows * lax.rsqrt(jnp.mean(rows * rows, -1, keepdims=True) + eps) * gain[...]).astype(BF16)

    @pl.when(here == 0)
    def _():
        edge = norm(halo[...])
        before[:, :width] = dot(edge, w_inner[...])[EDGE - 8 :]
        before[:, width:] = dot(edge, w_bc[...])[EDGE - 8 :]
        state[...] = jnp.zeros_like(state)
        passed[...] = jnp.zeros_like(passed)

    normed = norm(x[...])
    normed_o[...] = normed
    gate_o[...] = dot(normed, w_gate[...])
    pre = jnp.concatenate([dot(normed, w_inner[...]), dot(normed, w_bc[...])], 1)
    pre_o[...] = pre
    raw = dot(normed, w_step[...])
    raw_o[...] = raw
    padded = jnp.concatenate([before[...], pre], 0)
    kernel = taps.shape[0]
    first = 8 - (kernel - 1)
    total = bias[...] + sum(taps[k : k + 1, :] * padded[first + k : first + k + length] for k in range(kernel))
    before[...] = pre[length - 8 :]
    tot_o[...] = total
    inner = silu(total[:, :width])
    keys = silu(total[:, width : width + LANES]).astype(BF16)
    _, step = steps(raw, step_bias[...])
    rate = -jnp.exp(decay_log[...]) * step
    cum = dot_right(lower[...], rate)
    cum_o[...] = cum
    cum_rows_o[0] = cum.T[:8]
    last = cum[length - 1 : length]
    tail = widen(jnp.exp(last - cum) * step, spread[...])
    local = dot((tail * inner).astype(BF16), keys, 0, 0)
    local_o[0] = local
    state[...] = state_decay(last, spread[...]) * state[...] + local
    passed[...] = passed[...] + last
    write_payload(payload_o, state, passed)


def write_payload(payload_o, state, passed):
    width = state.shape[0]

    @pl.when(pl.program_id(0) == pl.num_programs(0) - 1)
    def _():
        coarse, fine = halves(state[...])
        payload_o[0, :width] = coarse
        payload_o[1, :width] = fine
        coarse, fine = halves(passed[...])
        payload_o[0, width:] = coarse
        payload_o[1, width:] = fine


def state_kernel(
    tot, raw, cum_in, cum_rows, gate, local, incoming, step_bias, skip, hide, spread,
    ssd_o, start_o, squares_o,
    state,
):
    width = gate.shape[1]

    @pl.when(pl.program_id(0) == 0)
    def _():
        state[...] = incoming[...]

    inner = silu(tot[:, :width])
    keys = silu(tot[:, width : width + LANES]).astype(BF16)
    queries = silu(tot[:, width + LANES :])
    _, step = steps(raw[...], step_bias[...])
    cum = cum_in[...]
    start = state[...]
    start_o[0] = start
    state[...] = state_decay(cum[cum.shape[0] - 1 :], spread[...]) * start + local[0]
    scores = dot_left(queries, keys, 1, 1)
    fed = (inner * widen(step, spread[...])).astype(BF16)
    carried = widen(jnp.exp(cum), spread[...]) * dot_both(queries, start, 1, 1)
    head_dim = width // HEADS_OF(width)
    outs = []
    for begin in range(0, width, LANES):
        size = min(LANES, width - begin)
        pair = fed[:, begin : begin + size]
        lane = lax.broadcasted_iota(jnp.int32, (1, size), 1)
        out = None
        for half in range(size // head_dim):
            h = begin // head_dim + half
            decay = jnp.exp(cum[:, h : h + 1] - cum_rows[0, h : h + 1, :] + hide[...])
            part = dot((scores * decay).astype(BF16), pair)
            out = part if out is None else jnp.where(lane < half * head_dim, out, part)
        outs.append(out)
    ssd = jnp.concatenate(outs, 1) + carried + skip[...] * inner
    ssd_o[...] = ssd
    mixed = ssd * silu(gate[...])
    squares_o[0] = as_rows(mixed * mixed)


HEAD_DIM = 64


def HEADS_OF(width):
    return width // HEAD_DIM


def scale_of(squares, width, all_width):
    return lax.rsqrt(as_columns(squares, width) / all_width + eps)


def out_kernel(all_width, ssd, gate, squares, gain, w_out, normed_o, part_o):
    width = ssd.shape[1]
    mixed = ssd[...] * silu(gate[...])
    normed = (mixed * scale_of(squares[0], width, all_width) * gain[...]).astype(BF16)
    normed_o[...] = normed
    for piece in range(w_out.shape[0]):
        part_o[piece] = dot(normed, w_out[piece]).astype(BF16)


def cross_kernel(pieces, *refs):
    grads, (w_out, ssd, gate, gain, dn_o, cross_o) = refs[:pieces], refs[pieces:]
    dn = sum(dot(grads[p][...], w_out[p], 1, 1) for p in range(pieces))
    dn_o[...] = dn
    cross_o[0] = as_rows(dn * gain[...] * (ssd[...] * silu(gate[...])))


def gate_kernel(pieces, all_width, *refs):
    grads = refs[:pieces]
    (
        ssd, gate, dn, tot, cum_in, normed, normed_out, squares, cross, gain, spread,
        dssd_o, dgate_o, local_o, payload_o, gw_out_o, gw_gate_o, sums_o,
        state, passed,
    ) = refs[pieces:]
    width, length = ssd.shape[1], ssd.shape[0]

    @pl.when(pl.program_id(0) == 0)
    def _():
        state[...] = jnp.zeros_like(state)
        passed[...] = jnp.zeros_like(passed)
        gw_out_o[...] = jnp.zeros_like(gw_out_o)
        gw_gate_o[...] = jnp.zeros_like(gw_gate_o)
        sums_o[...] = jnp.zeros_like(sums_o)

    g = gate[...]
    s = jax.nn.sigmoid(g)
    act = g * s
    mixed = ssd[...] * act
    scale = scale_of(squares[0], width, all_width)
    dscaled = dn[...] * scale
    along = as_columns(cross[0] / (squares[0] + all_width * eps), width)
    dmixed = scale * (dn[...] * gain[...] - mixed * along)
    dssd = dmixed * act
    dssd_o[...] = dssd
    dgate = (dmixed * ssd[...] * s * (1.0 + g * (1.0 - s))).astype(BF16)
    dgate_o[...] = dgate
    inner = silu(tot[:, :width])
    queries = silu(tot[:, width + LANES :])
    sums_o[0:1] = sums_o[0:1] + row_sum(dscaled * mixed)
    sums_o[1:2] = sums_o[1:2] + row_sum(dssd * inner)
    cum = cum_in[...]
    local = dot_both(widen(jnp.exp(cum), spread[...]) * dssd, queries, 0, 0)
    local_o[0] = local
    state[...] = state_decay(cum[length - 1 :], spread[...]) * state[...] + local
    passed[...] = passed[...] + cum[length - 1 :]
    for p in range(pieces):
        gw_out_o[p] = gw_out_o[p] + dot(normed_out[...], grads[p][...], 0, 0)
    gw_gate_o[...] = gw_gate_o[...] + dot(normed[...], dgate, 0, 0)
    write_payload(payload_o, state, passed)


def pull_kernel(
    tot, raw, cum_in, cum_rows, dssd, start, local, outgoing, step_bias, decay_log, skip, lower, hide, spread,
    d_o, draw_o, sums_o,
    state,
):
    width, length = dssd.shape[1], dssd.shape[0]

    @pl.when(pl.program_id(0) == 0)
    def _():
        state[...] = outgoing[...]
        sums_o[...] = jnp.zeros_like(sums_o)

    inner = silu(tot[:, :width])
    keys = silu(tot[:, width : width + LANES]).astype(BF16)
    queries = silu(tot[:, width + LANES :])
    shifted_raw, step = steps(raw[...], step_bias[...])
    rate = -jnp.exp(decay_log[...]) * step
    cum = cum_in[...]
    last = cum[length - 1 : length]
    ending = state[...]
    state[...] = state_decay(last, spread[...]) * ending + local[0]
    beginning = start[0]
    dy = dssd[...]
    dy16, dy_fine = halves(dy)
    ecum = jnp.exp(cum)
    tail = jnp.exp(last - cum)
    step_w = widen(step, spread[...])
    ecum_w = widen(ecum, spread[...])
    tail_w = widen(tail * step, spread[...])
    read = dot(queries.astype(BF16), beginning.astype(BF16), 1, 1)
    dqueries = dot_both(ecum_w * dy, beginning)
    taken = dot(keys, ending.astype(BF16), 1, 1)
    dkeys = dot_both(tail_w * inner, ending)
    from_start = ecum * narrow(dy * read, spread[...])
    to_end = tail * narrow(inner * taken, spread[...])
    both = as_rows(ending * beginning)
    through = jnp.exp(last) * narrow(both, spread[...])[0:1]
    scores = dot_left(queries, keys, 1, 1)
    fed, fed_fine = halves(inner * step_w)
    dscores = jnp.zeros_like(scores)
    crossing = jnp.zeros((length, LANES), F32)
    pulls, downs = [], []
    lanes_all = lax.broadcasted_iota(jnp.int32, (length, LANES), 1)
    for begin in range(0, width, LANES):
        size = min(LANES, width - begin)
        fed_pair, fed_low, dy_pair, dy_low = (v[:, begin : begin + size] for v in (fed, fed_fine, dy16, dy_fine))
        lane = lax.broadcasted_iota(jnp.int32, (1, size), 1)
        rows = []
        for half in range(size // HEAD_DIM):
            h = begin // HEAD_DIM + half
            inside = (lane >= half * HEAD_DIM) & (lane < (half + 1) * HEAD_DIM)
            fed_head = jnp.where(inside, fed_pair, jnp.zeros_like(fed_pair))
            low_head = jnp.where(inside, fed_low, jnp.zeros_like(fed_low))
            decay = jnp.exp(cum[:, h : h + 1] - cum_rows[0, h : h + 1, :] + hide[...])
            dweight = dot(dy_pair, fed_head, 1, 1) + dot(dy_low, fed_head, 1, 1) + dot(dy_pair, low_head, 1, 1)
            dweight = dweight * decay
            dscores = dscores + dweight
            weight = (scores * decay).astype(BF16)
            pulled = dot(dy_pair, weight, 0, 0)
            rows.append(pulled[half * HEAD_DIM : (half + 1) * HEAD_DIM])
            pair_terms = dweight * scores
            right = jnp.sum(pair_terms, 1, keepdims=True)
            downs.append(jnp.sum(pair_terms, 0, keepdims=True))
            crossing = jnp.where(lanes_all == h, right, crossing)
        pulls.append(jnp.concatenate(rows, 0).T)
    pulled = jnp.concatenate(pulls, 1)
    downs.append(jnp.zeros((LANES - len(downs), length), F32))
    crossing = crossing - jnp.concatenate(downs, 0).T
    coarse, fine = halves(dscores)
    dqueries = dqueries + dot(coarse, keys) + dot(fine, keys)
    dkeys = dkeys + (dot_left(queries, coarse, 0, 0) + dot(queries.astype(BF16), fine, 0, 0)).T
    dinner = (tail_w * taken + step_w * pulled) + skip[...] * dy
    dstep = narrow(inner * pulled, spread[...]) + to_end
    given = to_end * step
    drate = dot_right(lower[...], crossing + from_start, 0, 0) + (dot_right(lower[...], given) - given)
    drate = drate + through
    dstep = dstep - jnp.exp(decay_log[...]) * drate
    draw = dstep * jax.nn.sigmoid(shifted_raw)
    draw_o[...] = draw
    sums_o[0:1] = sums_o[0:1] + row_sum(draw)
    sums_o[1:2] = sums_o[1:2] + row_sum(rate * drate)
    d_o[:, :width] = dinner * silu_slope(tot[:, :width])
    d_o[:, width : width + LANES] = dkeys * silu_slope(tot[:, width : width + LANES])
    d_o[:, width + LANES :] = dqueries * silu_slope(tot[:, width + LANES :])


def project_kernel(
    d, halo, pre, normed, dgate, draw, taps, w_gate, w_inner, w_bc, w_step,
    part_o, gw_inner_o, gw_bc_o, gw_step_o, sums_o,
    after,
):
    width, length = w_gate.shape[1], d.shape[0]

    @pl.when(pl.program_id(0) == 0)
    def _():
        after[...] = halo[...]
        for out in (gw_inner_o, gw_bc_o, gw_step_o, sums_o):
            out[...] = jnp.zeros_like(out)

    kernel = taps.shape[0]
    grads = d[...]
    padded = jnp.concatenate([grads, after[...]], 0)
    after[...] = grads[:8]
    dpre = jnp.zeros_like(grads)
    for k in range(kernel):
        moved = padded[kernel - 1 - k : kernel - 1 - k + length]
        dpre = dpre + taps[k : k + 1, :] * moved
        sums_o[k : k + 1] = sums_o[k : k + 1] + row_sum(pre[...] * moved)
    sums_o[kernel : kernel + 1] = sums_o[kernel : kernel + 1] + row_sum(grads)
    dinner, dbc, dstep = dpre[:, :width].astype(BF16), dpre[:, width:], draw[...].astype(BF16)
    part = dot(dgate[...], w_gate[...], 1, 1) + dot(dinner, w_inner[...], 1, 1)
    part = part + dot_left(dbc, w_bc[...], 1, 1) + dot(dstep, w_step[...], 1, 1)
    part_o[...] = part.astype(BF16)
    gw_inner_o[...] = gw_inner_o[...] + dot(normed[...], dinner, 0, 0)
    gw_bc_o[...] = gw_bc_o[...] + dot_right(normed[...], dbc, 0, 0)
    gw_step_o[...] = gw_step_o[...] + dot(normed[...], dstep, 0, 0)


def call(kernel, blocks, ins, outs, scratch=(), backward=False, flops=10**9):
    def spec(shape, kind):
        def at(i):
            return blocks - 1 - i if backward else i

        if kind == "rows":
            return pl.BlockSpec((shape[0] // blocks,) + shape[1:], lambda i: (at(i), 0))
        if kind == "stack":
            return pl.BlockSpec((1,) + shape[1:], lambda i: (at(i), 0, 0))
        if kind == "mid":
            return pl.BlockSpec((shape[0], shape[1] // blocks, shape[2]), lambda i: (0, at(i), 0))
        return pl.BlockSpec(shape, lambda i: (0,) * len(shape))

    moved = sum(a.size * a.dtype.itemsize for a, _ in ins)
    return pl.pallas_call(
        kernel,
        grid=(blocks,),
        in_specs=[spec(a.shape, kind) for a, kind in ins],
        out_specs=[spec(shape, kind) for shape, _, kind in outs],
        out_shape=[jax.ShapeDtypeStruct(shape, dtype) for shape, dtype, _ in outs],
        scratch_shapes=[pltpu.VMEM(shape, F32) for shape in scratch],
        compiler_params=pltpu.CompilerParams(
            dimension_semantics=("arbitrary",), vmem_limit_bytes=48 * 1024 * 1024
        ),
        cost_estimate=pl.CostEstimate(flops=flops, bytes_accessed=moved, transcendentals=0),
    )(*[a for a, _ in ins])


def per_device(
    layer_input, gain_in, w_gate, w_inner, w_bc, w_step, conv_inner, conv_inner_bias, conv_bc, conv_bc_bias,
    step_bias, decay_log, skip_gain, gain_out, w_out, output_grad,
):
    count, features = layer_input.shape
    heads, width = decay_log.shape[0], w_gate.shape[1]
    states = w_bc.shape[1] // 2
    both = width + 2 * states
    blocks = count // BLOCK
    kernel = conv_inner.shape[0]
    pieces, mine = lax.axis_size("head"), lax.axis_index("head")
    all_width = width * pieces
    piece = output_grad.shape[1]
    rows = count // pieces
    heads_pad = ((0, 0), (0, LANES - heads))

    place = jnp.arange(BLOCK)
    keep = place[:, None] >= place[None, :]
    lower = keep.astype(BF16)
    hide = jnp.where(keep, 0.0, -1e30).astype(F32)
    spread = (jnp.arange(LANES)[:, None] == (jnp.arange(width) // (width // heads))[None, :]).astype(BF16)
    w_step_pad = jnp.pad(w_step, heads_pad)
    step_bias_pad = jnp.pad(step_bias[None], heads_pad)
    decay_pad = jnp.pad(decay_log[None], heads_pad)
    taps = jnp.concatenate([conv_inner, conv_bc], 1)
    bias = jnp.concatenate([conv_inner_bias, conv_bc_bias], 0)[None]
    skip = jnp.repeat(skip_gain, width // heads)[None]
    gain_out_row = gain_out[None]
    w_out_pieces = w_out.reshape(width, pieces, piece).transpose(1, 0, 2)
    owners = (mine - jnp.arange(pieces)) % pieces
    w_out_ring = jnp.take(w_out_pieces, owners, axis=0)

    halo = shifted(layer_input[count - EDGE :], "seq", 1)
    cotangents = ring_gather(output_grad, "head")

    whole = lambda *arrays: [(a, "whole") for a in arrays]
    normed, gate, pre, tot, raw, cum, cum_rows, local, payload = call(
        forward_kernel,
        blocks,
        [(layer_input, "rows")]
        + whole(halo, gain_in[None], w_gate, w_inner, w_bc, w_step_pad, taps, bias, step_bias_pad, decay_pad, lower, spread),
        [
            ((count, features), BF16, "rows"),
            ((count, width), F32, "rows"),
            ((count, both), F32, "rows"),
            ((count, both), F32, "rows"),
            ((count, LANES), F32, "rows"),
            ((count, LANES), F32, "rows"),
            ((blocks, 8, BLOCK), F32, "stack"),
            ((blocks, width, states), F32, "stack"),
            ((2, width + 16, states), BF16, "whole"),
        ],
        [(8, both), (width, states), (16, LANES)],
        flops=4 * 10**9,
    )
    incoming = joined_states(payload, "seq", width, heads, False)
    ssd, starts, squares = call(
        state_kernel,
        blocks,
        [(tot, "rows"), (raw, "rows"), (cum, "rows"), (cum_rows, "stack"), (gate, "rows"), (local, "stack")]
        + whole(incoming, step_bias_pad, skip, hide, spread),
        [
            ((count, width), F32, "rows"),
            ((blocks, width, states), F32, "stack"),
            ((blocks, 8, BLOCK), F32, "stack"),
        ],
        [(width, states)],
        flops=3 * 10**9,
    )
    squares = small_sum(squares, "head")
    normed_out, mixed_parts = call(
        functools.partial(out_kernel, all_width),
        blocks,
        [(ssd, "rows"), (gate, "rows"), (squares, "stack")] + whole(gain_out_row, w_out_pieces),
        [((count, width), BF16, "rows"), ((pieces, count, piece), BF16, "mid")],
        flops=2 * 10**9,
    )
    dn, cross = call(
        functools.partial(cross_kernel, pieces),
        blocks,
        [(c, "rows") for c in cotangents]
        + whole(w_out_ring)
        + [(ssd, "rows"), (gate, "rows")]
        + whole(gain_out_row),
        [((count, width), F32, "rows"), ((blocks, 8, BLOCK), F32, "stack")],
        flops=2 * 10**9,
    )
    cross = small_sum(cross, "head")
    summed = ring_scatter(lambda q: lax.dynamic_index_in_dim(mixed_parts, q, 0, False), "head")
    residual = lax.dynamic_slice_in_dim(layer_input, mine * piece, piece, 1).astype(F32)
    mixed = (residual + summed).astype(BF16)

    dssd, dgate, local_back, payload_back, gw_out, gw_gate, gate_sums = call(
        functools.partial(gate_kernel, pieces, all_width),
        blocks,
        [(c, "rows") for c in cotangents]
        + [(a, "rows") for a in (ssd, gate, dn, tot, cum, normed, normed_out)]
        + [(squares, "stack"), (cross, "stack")]
        + whole(gain_out_row, spread),
        [
            ((count, width), F32, "rows"),
            ((count, width), BF16, "rows"),
            ((blocks, width, states), F32, "stack"),
            ((2, width + 16, states), BF16, "whole"),
            ((pieces, width, piece), F32, "whole"),
            ((features, width), F32, "whole"),
            ((8, width), F32, "whole"),
        ],
        [(width, states), (16, LANES)],
        backward=True,
        flops=4 * 10**9,
    )
    gw_out, gw_gate = lax.psum((gw_out, gw_gate), "seq")
    outgoing = joined_states(payload_back, "seq", width, heads, True)
    d, draw, rate_sums = call(
        pull_kernel,
        blocks,
        [(tot, "rows"), (raw, "rows"), (cum, "rows"), (cum_rows, "stack"), (dssd, "rows"), (starts, "stack"), (local_back, "stack")]
        + whole(outgoing, step_bias_pad, decay_pad, skip, lower, hide, spread),
        [((count, both), F32, "rows"), ((count, LANES), F32, "rows"), ((8, LANES), F32, "whole")],
        [(width, states)],
        backward=True,
        flops=8 * 10**9,
    )
    d_halo = shifted(d[:8], "seq", -1)
    part, gw_inner, gw_bc, gw_step, conv_sums = call(
        project_kernel,
        blocks,
        [(d, "rows")]
        + whole(d_halo)
        + [(pre, "rows"), (normed, "rows"), (dgate, "rows"), (draw, "rows")]
        + whole(taps, w_gate, w_inner, w_bc, w_step_pad),
        [
            ((count, features), BF16, "rows"),
            ((features, width), F32, "whole"),
            ((features, 2 * states), F32, "whole"),
            ((features, LANES), F32, "whole"),
            ((8, both), F32, "whole"),
        ],
        [(8, both)],
        backward=True,
        flops=8 * 10**9,
    )
    dnormed = ring_scatter(lambda q: lax.dynamic_slice_in_dim(part, q * rows, rows, 0), "head")

    layer_x = lax.dynamic_slice_in_dim(layer_input, mine * rows, rows, 0).astype(F32)
    own = [lax.dynamic_slice_in_dim(c, mine * rows, rows, 0) for c in cotangents]
    cotangent = jnp.take(jnp.stack(own), owners, axis=0).transpose(1, 0, 2).reshape(rows, features).astype(F32)
    scale_in = lax.rsqrt(jnp.mean(layer_x * layer_x, -1, keepdims=True) + eps)
    scaled_in = dnormed * gain_in
    gain_part = jnp.sum(dnormed * layer_x * scale_in, 0)
    own_input = scaled_in * scale_in - layer_x * scale_in**3 * jnp.mean(scaled_in * layer_x, -1, keepdims=True)
    own_input = (own_input + cotangent).astype(BF16)
    grad_input = jnp.zeros((count, features), F32)
    for step, block in enumerate(ring_gather(own_input, "head")):
        owner = (mine - step) % pieces
        grad_input = lax.dynamic_update_slice_in_dim(grad_input, block.astype(F32), owner * rows, 0)

    gw_out = jnp.take(gw_out, owners, axis=0).transpose(1, 0, 2).reshape(width, features)
    (gw_inner, gw_bc, gw_step), gw_gate, gw_out = lax.optimization_barrier(
        ((gw_inner, gw_bc, gw_step), gw_gate, gw_out)
    )
    gw_inner, gw_bc, gw_step = lax.psum((gw_inner, gw_bc, gw_step[:, :heads]), "seq")
    seq_count, seq_mine = lax.axis_size("seq"), lax.axis_index("seq")
    share = features // seq_count
    bc_share = lax.dynamic_slice_in_dim(gw_bc, seq_mine * share, share, 0)
    gw_bc = lax.all_gather(small_sum(bc_share, "head"), "seq", axis=0, tiled=True)
    small = [conv_sums, gate_sums, rate_sums]
    packed = butterfly(jnp.concatenate([v.reshape(-1, LANES) for v in small], 0), "seq")
    split, at = [], 0
    for v in small:
        split.append(packed[at : at + v.size // LANES].reshape(v.shape))
        at += v.size // LANES
    conv_sums, gate_sums, rate_sums = split
    shared = jnp.concatenate([v.reshape(-1, LANES) for v in (conv_sums[:, width:] / seq_count, gain_part)], 0)
    shared = butterfly(butterfly(shared, "seq"), "head")
    bc_sums, grad_gain_in = shared[: 4 * states // LANES * 4].reshape(8, 2 * states), shared[16 * states // LANES :].reshape(-1)
    head_dim = width // heads
    return (
        mixed,
        grad_input,
        grad_gain_in,
        gw_gate,
        gw_inner,
        gw_bc,
        gw_step,
        conv_sums[:kernel, :width],
        conv_sums[kernel, :width],
        bc_sums[:kernel],
        bc_sums[kernel],
        rate_sums[0, :heads],
        rate_sums[1, :heads],
        gate_sums[1].reshape(heads, head_dim).sum(1),
        gate_sums[0],
        gw_out,
    )


def solution(mesh):
    placed = (
        P("seq", None),
        P(),
        P(None, "head"),
        P(None, "head"),
        P(),
        P(None, "head"),
        P(None, "head"),
        P("head"),
        P(),
        P(),
        P("head"),
        P("head"),
        P("head"),
        P("head"),
        P("head", None),
        P("seq", "head"),
    )
    return jax.shard_map(
        per_device,
        mesh=mesh,
        in_specs=placed,
        out_specs=(
            P("seq", "head"),
            P("seq", None),
            P(),
            P(None, "head"),
            P(None, "head"),
            P(),
            P(None, "head"),
            P(None, "head"),
            P("head"),
            P(),
            P(),
            P("head"),
            P("head"),
            P("head"),
            P("head"),
            P("head", None),
        ),
        check_vma=False,
    )
```

```python
import functools
import jax
import jax.numpy as jnp
import numpy as np
from jax import lax
from jax.experimental import pallas as pl
from jax.experimental.pallas import tpu as pltpu
from jax.sharding import PartitionSpec as P

BLOCK = 256
LANES = 128
EDGE = 16
F32, BF16 = jnp.float32, jnp.bfloat16
eps = 1e-05


def turn(block, axis, distance):
    count = lax.axis_size(axis)
    return lax.ppermute(block, axis, [(i, (i + distance) % count) for i in range(count)])


def shifted(block, axis, distance):
    devices = range(lax.axis_size(axis))
    return lax.ppermute(block, axis, [(i - distance, i) for i in devices if i - distance in devices])


def tie(*values):
    return lax.optimization_barrier(values)


def ring_scatter(parts, axis):
    count, mine = lax.axis_size(axis), lax.axis_index(axis)
    total = parts((mine - 1) % count)
    for step in range(count - 1):
        arrived = yield turn(total, axis, 1)
        total = arrived.astype(F32) + parts((mine - 2 - step) % count).astype(F32)
        if step < count - 2:
            total = total.astype(BF16)
    yield total


def halved(value, axis, reach):
    count, mine = lax.axis_size(axis), lax.axis_index(axis)
    pair = value.reshape(2, value.shape[0] // 2, value.shape[1])
    bit = (mine // reach) % 2
    sent = lax.dynamic_index_in_dim(pair, 1 - bit, 0, False)
    kept = lax.dynamic_index_in_dim(pair, bit, 0, False)
    return kept + lax.ppermute(sent, axis, [(i, i ^ reach) for i in range(count)])


def doubled(value, axis, reach):
    count, mine = lax.axis_size(axis), lax.axis_index(axis)
    other = lax.ppermute(value, axis, [(i, i ^ reach) for i in range(count)])
    second = (mine // reach) % 2 == 1
    return jnp.where(second, jnp.concatenate([other, value], 0), jnp.concatenate([value, other], 0))


def swapped_sum(value, axis, reach):
    return value + lax.ppermute(value, axis, [(i, i ^ reach) for i in range(lax.axis_size(axis))])


def reaches(axis):
    reach, found = 1, []
    while reach < lax.axis_size(axis):
        found.append(reach)
        reach *= 2
    return found


def weight_chores(gw_inner, gw_bc, sums, width):
    for reach in reaches("seq"):
        gw_inner, gw_bc, sums = yield (
            halved(gw_inner, "seq", reach),
            halved(gw_bc, "seq", reach),
            swapped_sum(sums, "seq", reach),
        )
    share = gw_bc.shape[0]
    mine = jnp.concatenate([gw_bc, sums[:8, width : width + gw_bc.shape[1]]], 0)
    shared, gw_inner = yield small_sum(mine, "head"), gw_inner
    gw_bc, bc_sums = shared[:share], shared[share:]
    for reach in reaches("seq")[::-1]:
        gw_inner, gw_bc = yield doubled(gw_inner, "seq", reach), doubled(gw_bc, "seq", reach)
    yield gw_inner, gw_bc, sums, bc_sums


def gain_chores(gain_part):
    gain_part = yield (small_sum(gain_part[0], "head"),)
    for reach in reaches("seq"):
        gain_part = yield (swapped_sum(gain_part[0], "seq", reach),)


class Chores:
    def __init__(self, steps):
        self.steps, self.state = steps, next(steps)

    def beside(self, running):
        if self.steps is not None:
            running, *state = tie(running, *self.state)
            self.advance(tuple(state))
        return running

    def advance(self, state):
        try:
            self.state = self.steps.send(state)
        except StopIteration:
            self.state, self.steps = state, None

    def finish(self):
        while self.steps is not None:
            self.advance(self.state)
        return self.state


def small_sum(value, axis):
    total = value
    for step in range(1, lax.axis_size(axis)):
        total = total + turn(value, axis, step)
    return total


def joined_states(pieces, axis, width, heads, backward, fine=None):
    count, mine = lax.axis_size(axis), lax.axis_index(axis)
    pieces = pieces.astype(F32)
    logs = pieces[:, width, :heads] + pieces[:, width + 8, :heads]
    states = pieces[:, :width]
    if fine is not None:
        states = states + fine.astype(F32)
    place = jnp.arange(count)
    k, m = place[:, None], place[None, :]
    if backward:
        between, counted = (m > mine) & (m < k), place > mine
    else:
        between, counted = (m > k) & (m < mine), place < mine
    passed = jnp.sum(jnp.where(between[:, :, None], logs[None], 0.0), 1)
    weight = jnp.where(counted[:, None], jnp.exp(passed), 0.0)
    weight = jnp.repeat(weight, width // heads, 1)
    return jnp.sum(weight[:, :, None] * states, 0)


def dot(left, right, left_dim=1, right_dim=0, precision=None):
    return lax.dot_general(
        left, right, (((left_dim,), (right_dim,)), ((), ())), precision=precision, preferred_element_type=F32
    )


def silu(value):
    return value * jax.nn.sigmoid(value)


def silu_slope(value):
    s = jax.nn.sigmoid(value)
    return s * (1.0 + value * (1.0 - s))


def halves(value):
    coarse = value.astype(BF16)
    return coarse, (value - coarse.astype(F32)).astype(BF16)


def dot_left(left, right, left_dim=1, right_dim=0):
    coarse, fine = halves(left)
    return dot(coarse, right, left_dim, right_dim) + dot(fine, right, left_dim, right_dim)


def dot_right(left, right, left_dim=1, right_dim=0):
    coarse, fine = halves(right)
    return dot(left, coarse, left_dim, right_dim) + dot(left, fine, left_dim, right_dim)


def dot_both(left, right, left_dim=1, right_dim=0):
    coarse, fine = halves(left)
    return dot_right(coarse, right, left_dim, right_dim) + dot(fine, right.astype(BF16), left_dim, right_dim)


def steps(raw, step_bias):
    moved = raw + step_bias
    return moved, jnp.maximum(moved, 0.0) + jnp.log1p(jnp.exp(-jnp.abs(moved)))


def widen(value, spread):
    return dot_left(value, spread)


def narrow(value, spread):
    return dot_left(value, spread, 1, 1)


def state_decay(last, spread):
    return dot_right(spread, jnp.broadcast_to(jnp.exp(last), (LANES, LANES)).T, 0, 0)


def as_columns(rows, width):
    return dot_left(rows, jnp.full((rows.shape[0], width), 1.0 / rows.shape[0], BF16), 0, 0)


def as_rows(value):
    return dot_right(jnp.ones((8, value.shape[1]), BF16), value, 1, 1)


def row_sum(value):
    return jnp.sum(value, 0, keepdims=True)


def forward_kernel(
    x, halo, gain, w_gate, w_inner, w_bc, w_step, taps_a, taps_b, bias_a, bias_b, step_bias, decay_log, lower, spread,
    normed_o, gate_o, pre_o, tot_o, raw_o, cum_o, cum_rows_o, local_o, payload_o, fine_o,
    before, state, passed,
):
    here, length, width = pl.program_id(0), x.shape[0], w_gate.shape[1]

    def norm(rows):
        rows = rows.astype(F32)
        return (rows * lax.rsqrt(jnp.mean(rows * rows, -1, keepdims=True) + eps) * gain[...]).astype(BF16)

    @pl.when(here == 0)
    def _():
        edge = norm(halo[...])
        before[:, :width] = dot(edge, w_inner[...])[EDGE - 8 :]
        before[:, width:] = dot(edge, w_bc[...])[EDGE - 8 :]
        state[...] = jnp.zeros_like(state)
        passed[...] = jnp.zeros_like(passed)

    normed = norm(x[...])
    normed_o[...] = normed
    gate_o[...] = dot(normed, w_gate[...])
    pre = jnp.concatenate([dot(normed, w_inner[...]), dot(normed, w_bc[...])], 1)
    pre_o[...] = pre
    raw = padded_row(dot(normed, w_step[...]))
    raw_o[...] = raw
    padded = jnp.concatenate([before[...], pre], 0)
    taps = jnp.concatenate([taps_a[...], taps_b[...]], 1)
    kernel = taps.shape[0]
    first = 8 - (kernel - 1)
    total = jnp.concatenate([bias_a[...], bias_b[...]], 1) + sum(taps[k : k + 1, :] * padded[first + k : first + k + length] for k in range(kernel))
    before[...] = pre[length - 8 :]
    tot_o[...] = total
    inner = silu(total[:, :width])
    keys = silu(total[:, width : width + LANES]).astype(BF16)
    _, step = steps(raw, padded_row(step_bias[...]))
    rate = -jnp.exp(padded_row(decay_log[...])) * step
    cum = dot_right(lower[...], rate)
    cum_o[...] = cum
    cum_rows_o[0] = cum.T[:8]
    last = cum[length - 1 : length]
    tail = widen(jnp.exp(last - cum) * step, spread[...])
    local = dot((tail * inner).astype(BF16), keys, 0, 0)
    local_o[0] = local
    state[...] = state_decay(last, spread[...]) * state[...] + local
    passed[...] = passed[...] + last
    write_payload(payload_o, state, passed, fine_o)


def padded_row(row):
    return jnp.concatenate([row, jnp.zeros((row.shape[0], LANES - row.shape[1]), F32)], 1)


def skip_row(skip, spread):
    return widen(jnp.broadcast_to(padded_row(skip[...]), (8, LANES)), spread[...])[0:1]


def write_payload(payload_o, state, passed, fine_o=None):
    width = state.shape[0]

    @pl.when(pl.program_id(0) == pl.num_programs(0) - 1)
    def _():
        payload_o[:width] = state[...].astype(BF16)
        coarse = passed[:8].astype(BF16).astype(F32)
        payload_o[width : width + 16] = jnp.concatenate([coarse, passed[:8] - coarse], 0).astype(BF16)
        if fine_o is not None:
            fine_o[...] = halves(state[...])[1]


def state_kernel(
    tot, raw, cum_in, cum_rows, gate, local, incoming, step_bias, skip, hide, spread,
    ssd_o, start_o, squares_o,
    state,
):
    width = gate.shape[1]

    @pl.when(pl.program_id(0) == 0)
    def _():
        state[...] = incoming[...]

    inner = silu(tot[:, :width])
    keys = silu(tot[:, width : width + LANES]).astype(BF16)
    queries = silu(tot[:, width + LANES :])
    _, step = steps(raw[...], padded_row(step_bias[...]))
    cum = cum_in[...]
    start = state[...]
    start_o[0] = start
    state[...] = state_decay(cum[cum.shape[0] - 1 :], spread[...]) * start + local[0]
    scores = dot_left(queries, keys, 1, 1)
    fed = (inner * widen(step, spread[...])).astype(BF16)
    carried = widen(jnp.exp(cum), spread[...]) * dot_both(queries, start, 1, 1)
    head_dim = width // HEADS_OF(width)
    outs = []
    for begin in range(0, width, LANES):
        size = min(LANES, width - begin)
        pair = fed[:, begin : begin + size]
        lane = lax.broadcasted_iota(jnp.int32, (1, size), 1)
        out = None
        for half in range(size // head_dim):
            h = begin // head_dim + half
            decay = jnp.exp(cum[:, h : h + 1] - cum_rows[0, h : h + 1, :] + hide[...])
            part = dot((scores * decay).astype(BF16), pair)
            out = part if out is None else jnp.where(lane < half * head_dim, out, part)
        outs.append(out)
    ssd = jnp.concatenate(outs, 1) + carried + skip_row(skip, spread) * inner
    ssd_o[...] = ssd
    mixed = ssd * silu(gate[...])
    squares_o[0] = as_rows(mixed * mixed)


HEAD_DIM = 64


def HEADS_OF(width):
    return width // HEAD_DIM


def scale_of(squares, width, all_width):
    return lax.rsqrt(as_columns(squares, width) / all_width + eps)


def out_kernel(all_width, ssd, gate, squares, gain, w_out, normed_o, part_o):
    width = ssd.shape[1]
    mixed = ssd[...] * silu(gate[...])
    normed = (mixed * scale_of(squares[0], width, all_width) * gain[...]).astype(BF16)
    normed_o[...] = normed
    for piece in range(w_out.shape[0]):
        part_o[piece] = dot(w_out[piece], normed, 1, 1).astype(BF16)


def cross_kernel(pieces, *refs):
    grads, (w_out, ssd, gate, gain, dn_o, cross_o) = refs[:pieces], refs[pieces:]
    dn = sum(dot(grads[p][...], w_out[p], 0, 0) for p in range(pieces))
    dn_o[...] = dn
    cross_o[0] = as_rows(dn * gain[...] * (ssd[...] * silu(gate[...])))


def gate_kernel(pieces, all_width, *refs):
    grads = refs[:pieces]
    (
        ssd, gate, dn, tot, cum_in, normed, normed_out, squares, cross, gain, spread,
        dssd_o, dgate_o, local_o, payload_o, gw_out_o, gw_gate_o, sums_o,
        state, passed,
    ) = refs[pieces:]
    width, length = ssd.shape[1], ssd.shape[0]

    @pl.when(pl.program_id(0) == 0)
    def _():
        state[...] = jnp.zeros_like(state)
        passed[...] = jnp.zeros_like(passed)
        gw_out_o[...] = jnp.zeros_like(gw_out_o)
        gw_gate_o[...] = jnp.zeros_like(gw_gate_o)
        sums_o[...] = jnp.zeros_like(sums_o)

    g = gate[...]
    s = jax.nn.sigmoid(g)
    act = g * s
    mixed = ssd[...] * act
    scale = scale_of(squares[0], width, all_width)
    dscaled = dn[...] * scale
    along = as_columns(cross[0] / (squares[0] + all_width * eps), width)
    dmixed = scale * (dn[...] * gain[...] - mixed * along)
    dssd = dmixed * act
    dssd_o[...] = dssd
    dgate = (dmixed * ssd[...] * s * (1.0 + g * (1.0 - s))).astype(BF16)
    dgate_o[...] = dgate
    inner = silu(tot[:, :width])
    queries = silu(tot[:, width + LANES :])
    sums_o[0:1] = sums_o[0:1] + row_sum(dscaled * mixed)
    sums_o[1:2] = sums_o[1:2] + row_sum(dssd * inner)
    cum = cum_in[...]
    local = dot_both(widen(jnp.exp(cum), spread[...]) * dssd, queries, 0, 0)
    local_o[0] = local
    state[...] = state_decay(cum[length - 1 :], spread[...]) * state[...] + local
    passed[...] = passed[...] + cum[length - 1 :]
    for p in range(pieces):
        gw_out_o[p] = gw_out_o[p] + dot(grads[p][...], normed_out[...])
    gw_gate_o[...] = gw_gate_o[...] + dot(normed[...], dgate, 0, 0)
    write_payload(payload_o, state, passed)


def pull_kernel(
    tot, raw, cum_in, cum_rows, dssd, start, local, outgoing, step_bias, decay_log, skip, lower, hide, spread,
    d_o, draw_o, sums_o,
    state,
):
    width, length = dssd.shape[1], dssd.shape[0]

    @pl.when(pl.program_id(0) == 0)
    def _():
        state[...] = outgoing[...]
        sums_o[...] = jnp.zeros_like(sums_o)

    inner = silu(tot[:, :width])
    keys = silu(tot[:, width : width + LANES]).astype(BF16)
    queries = silu(tot[:, width + LANES :])
    shifted_raw, step = steps(raw[...], padded_row(step_bias[...]))
    growth = jnp.exp(padded_row(decay_log[...]))
    rate = -growth * step
    cum = cum_in[...]
    last = cum[length - 1 : length]
    ending = state[...]
    state[...] = state_decay(last, spread[...]) * ending + local[0]
    beginning = start[0]
    dy = dssd[...]
    dy16, dy_fine = halves(dy)
    ecum = jnp.exp(cum)
    tail = jnp.exp(last - cum)
    step_w = widen(step, spread[...])
    ecum_w = widen(ecum, spread[...])
    tail_w = widen(tail * step, spread[...])
    read = dot(queries.astype(BF16), beginning.astype(BF16), 1, 1)
    dqueries = dot_both(ecum_w * dy, beginning)
    taken = dot(keys, ending.astype(BF16), 1, 1)
    dkeys = dot_both(tail_w * inner, ending)
    from_start = ecum * narrow(dy * read, spread[...])
    to_end = tail * narrow(inner * taken, spread[...])
    both = as_rows(ending * beginning)
    through = jnp.exp(last) * narrow(both, spread[...])[0:1]
    scores = dot_left(queries, keys, 1, 1)
    fed, fed_fine = halves(inner * step_w)
    dscores = jnp.zeros_like(scores)
    crossing = jnp.zeros((length, LANES), F32)
    pulls, downs = [], []
    lanes_all = lax.broadcasted_iota(jnp.int32, (length, LANES), 1)
    for begin in range(0, width, LANES):
        size = min(LANES, width - begin)
        fed_pair, fed_low, dy_pair, dy_low = (v[:, begin : begin + size] for v in (fed, fed_fine, dy16, dy_fine))
        lane = lax.broadcasted_iota(jnp.int32, (1, size), 1)
        rows = []
        for half in range(size // HEAD_DIM):
            h = begin // HEAD_DIM + half
            inside = (lane >= half * HEAD_DIM) & (lane < (half + 1) * HEAD_DIM)
            fed_head = jnp.where(inside, fed_pair, jnp.zeros_like(fed_pair))
            low_head = jnp.where(inside, fed_low, jnp.zeros_like(fed_low))
            decay = jnp.exp(cum[:, h : h + 1] - cum_rows[0, h : h + 1, :] + hide[...])
            dweight = dot(dy_pair, fed_head, 1, 1) + dot(dy_low, fed_head, 1, 1) + dot(dy_pair, low_head, 1, 1)
            dweight = dweight * decay
            dscores = dscores + dweight
            weight = (scores * decay).astype(BF16)
            pulled = dot(dy_pair, weight, 0, 0)
            rows.append(pulled[half * HEAD_DIM : (half + 1) * HEAD_DIM])
            pair_terms = dweight * scores
            right = jnp.sum(pair_terms, 1, keepdims=True)
            downs.append(jnp.sum(pair_terms, 0, keepdims=True))
            crossing = jnp.where(lanes_all == h, right, crossing)
        pulls.append(jnp.concatenate(rows, 0).T)
    pulled = jnp.concatenate(pulls, 1)
    downs.append(jnp.zeros((LANES - len(downs), length), F32))
    crossing = crossing - jnp.concatenate(downs, 0).T
    coarse, fine = halves(dscores)
    dqueries = dqueries + dot(coarse, keys) + dot(fine, keys)
    dkeys = dkeys + (dot_left(queries, coarse, 0, 0) + dot(queries.astype(BF16), fine, 0, 0)).T
    dinner = (tail_w * taken + step_w * pulled) + skip_row(skip, spread) * dy
    dstep = narrow(inner * pulled, spread[...]) + to_end
    given = to_end * step
    drate = dot_right(lower[...], crossing + from_start, 0, 0) + (dot_right(lower[...], given) - given)
    drate = drate + through
    dstep = dstep - growth * drate
    draw = dstep * jax.nn.sigmoid(shifted_raw)
    draw_o[...] = draw
    sums_o[0:1] = sums_o[0:1] + row_sum(draw)
    sums_o[1:2] = sums_o[1:2] + row_sum(rate * drate)
    d_o[:, :width] = dinner * silu_slope(tot[:, :width])
    d_o[:, width : width + LANES] = dkeys * silu_slope(tot[:, width : width + LANES])
    d_o[:, width + LANES :] = dqueries * silu_slope(tot[:, width + LANES :])


def project_kernel(
    earlier, d, halo, pre, normed, dgate, draw, gate_sums, rate_sums, taps_a, taps_b, w_gate, w_inner, w_bc, w_step, *refs
):
    given, (part_o, *totals, after) = refs[:earlier], refs[earlier:]
    gw_inner_o, gw_bc_o, sums_o = totals
    width, length = w_gate.shape[1], d.shape[0]

    @pl.when(pl.program_id(0) == 0)
    def _():
        after[...] = halo[...]
        for at, out in enumerate(totals):
            out[...] = given[at][...] if earlier else jnp.zeros_like(out)
        if not earlier:
            rows = jnp.concatenate([gate_sums[0:2], rate_sums[0:2], jnp.zeros((2, LANES), F32)], 1)
            sums_o[taps_a.shape[0] + 1 : taps_a.shape[0] + 3, : rows.shape[1]] = rows

    taps = jnp.concatenate([taps_a[...], taps_b[...]], 1)
    kernel, heads, both = taps.shape[0], w_step.shape[1], taps.shape[1]
    features = normed.shape[1]
    grads = d[...]
    padded = jnp.concatenate([grads, after[...]], 0)
    after[...] = grads[:8]
    dpre = jnp.zeros_like(grads)
    for k in range(kernel):
        moved = padded[kernel - 1 - k : kernel - 1 - k + length]
        dpre = dpre + taps[k : k + 1, :] * moved
        sums_o[k : k + 1, :both] = sums_o[k : k + 1, :both] + row_sum(pre[...] * moved)
    sums_o[kernel : kernel + 1, :both] = sums_o[kernel : kernel + 1, :both] + row_sum(grads)
    dinner, dbc, dstep = dpre[:, :width].astype(BF16), dpre[:, width:], draw[:, :heads].astype(BF16)
    part = dot(dgate[...], w_gate[...], 1, 1) + dot(dinner, w_inner[...], 1, 1)
    part = part + dot_left(dbc, w_bc[...], 1, 1) + dot(dstep, w_step[...], 1, 1)
    part_o[...] = part.astype(BF16)
    gw_inner_o[...] = gw_inner_o[...] + dot(normed[...], dinner, 0, 0)
    gw_bc_o[...] = gw_bc_o[...] + dot_right(normed[...], dbc, 0, 0)
    sums_o[8 : 8 + heads, :features] = sums_o[8 : 8 + heads, :features] + dot(dstep, normed[...], 0, 0)


def input_kernel(place, dnormed, x, gain, *refs):
    pieces = len(refs) - 3
    grads, (block_o, sums_o, columns) = refs[:pieces], refs[pieces:]
    for p in range(pieces):
        columns[(place[0] - p + pieces) % pieces] = grads[p][...].astype(F32)
    cotangent = jnp.concatenate([columns[q] for q in range(pieces)], 0).T
    rows = x[...].astype(F32)
    scale = lax.rsqrt(jnp.mean(rows * rows, -1, keepdims=True) + eps)
    scaled = dnormed[...] * gain[...]
    sums_o[...] = jnp.broadcast_to(row_sum(dnormed[...] * rows * scale), sums_o.shape)
    along = rows * (scale * scale * scale * jnp.mean(scaled * rows, -1, keepdims=True))
    block_o[...] = (scaled * scale - along + cotangent).astype(BF16)


def input_call(mine, side, dnormed, layer_input, gain, cotangents):
    rows, features = dnormed.shape
    pieces = len(cotangents)
    piece = cotangents[0].shape[0]
    return pl.pallas_call(
        input_kernel,
        grid_spec=pltpu.PrefetchScalarGridSpec(
            num_scalar_prefetch=1,
            grid=(1,),
            in_specs=[
                pl.BlockSpec((rows, features), lambda i, place: (0, 0)),
                pl.BlockSpec((rows, features), lambda i, place: (side * pieces + place[0], 0)),
                pl.BlockSpec((1, features), lambda i, place: (0, 0)),
            ]
            + [pl.BlockSpec((piece, rows), lambda i, place: (0, side * pieces + place[0]))] * pieces,
            out_specs=[
                pl.BlockSpec((rows, features), lambda i, place: (0, 0)),
                pl.BlockSpec((8, features), lambda i, place: (0, 0)),
            ],
            scratch_shapes=[pltpu.VMEM((pieces, piece, rows), F32)],
        ),
        out_shape=[jax.ShapeDtypeStruct((rows, features), BF16), jax.ShapeDtypeStruct((8, features), F32)],
        compiler_params=pltpu.CompilerParams(
            dimension_semantics=("arbitrary",), vmem_limit_bytes=60 * 1024 * 1024
        ),
        cost_estimate=pl.CostEstimate(flops=10**6, bytes_accessed=10**4, transcendentals=0),
    )(mine[None].astype(jnp.int32), dnormed, layer_input, gain, *cotangents)


def assemble_kernel(place, *refs):
    blocks, out = refs[:-1], refs[-1]
    pieces = len(blocks) // 2
    here = pl.program_id(0)
    wanted = here // pieces * pieces + (place[0] - here % pieces + pieces) % pieces
    for at, block in enumerate(blocks):

        @pl.when(wanted == at)
        def _():
            out[...] = block[...].astype(F32)


def assemble_call(mine, blocks):
    rows, features = blocks[0].shape
    return pl.pallas_call(
        assemble_kernel,
        grid_spec=pltpu.PrefetchScalarGridSpec(
            num_scalar_prefetch=1,
            grid=(len(blocks),),
            in_specs=[pl.BlockSpec((rows, features), lambda i, place: (0, 0))] * len(blocks),
            out_specs=pl.BlockSpec((rows, features), lambda i, place: (i, 0)),
        ),
        out_shape=jax.ShapeDtypeStruct((rows * len(blocks), features), F32),
        compiler_params=pltpu.CompilerParams(
            dimension_semantics=("arbitrary",), vmem_limit_bytes=60 * 1024 * 1024
        ),
        cost_estimate=pl.CostEstimate(flops=10**6, bytes_accessed=10**4, transcendentals=0),
    )(mine[None].astype(jnp.int32), *blocks)


def call(kernel, blocks, ins, outs, scratch=(), backward=False, total=None, skipped=0):
    steps_here = blocks

    def spec(shape, kind, blocks=blocks, skipped=0):
        def at(i):
            return skipped + (steps_here - 1 - i if backward else i)

        if kind == "rows":
            return pl.BlockSpec((shape[0] // blocks,) + shape[1:], lambda i: (at(i), 0))
        if kind == "stack":
            return pl.BlockSpec((1,) + shape[1:], lambda i: (at(i), 0, 0))
        if kind == "columns":
            return pl.BlockSpec((shape[0], shape[1] // blocks), lambda i: (0, at(i)))
        if kind == "last":
            return pl.BlockSpec((shape[0], shape[1], shape[2] // blocks), lambda i: (0, 0, at(i)))
        return pl.BlockSpec(shape, lambda i: (0,) * len(shape))

    return pl.pallas_call(
        kernel,
        grid=(blocks,),
        in_specs=[spec(a.shape, kind, total or blocks, skipped) for a, kind in ins],
        out_specs=[spec(shape, kind) for shape, _, kind in outs],
        out_shape=[jax.ShapeDtypeStruct(shape, dtype) for shape, dtype, _ in outs],
        scratch_shapes=[pltpu.VMEM(shape, F32) for shape in scratch],
        compiler_params=pltpu.CompilerParams(
            dimension_semantics=("arbitrary",), vmem_limit_bytes=60 * 1024 * 1024
        ),
        cost_estimate=pl.CostEstimate(flops=10**6, bytes_accessed=10**4, transcendentals=0),
    )(*[a for a, _ in ins])


def per_device(
    layer_input, gain_in, w_gate, w_inner, w_bc, w_step, conv_inner, conv_inner_bias, conv_bc, conv_bc_bias,
    step_bias, decay_log, skip_gain, gain_out, w_out, output_grad,
):
    count, features = layer_input.shape
    heads, width = decay_log.shape[0], w_gate.shape[1]
    states = w_bc.shape[1] // 2
    both = width + 2 * states
    blocks = count // BLOCK
    kernel = conv_inner.shape[0]
    pieces, mine = lax.axis_size("head"), lax.axis_index("head")
    all_width = width * pieces
    piece = output_grad.shape[1]
    rows = count // pieces

    place = np.arange(BLOCK)
    keep = place[:, None] >= place[None, :]
    lower = jnp.asarray(keep, BF16)
    hide = jnp.asarray(np.where(keep, 0.0, -1e30), F32)
    spread = jnp.asarray(np.arange(LANES)[:, None] == (np.arange(width) // (width // heads))[None, :], BF16)
    bias_row, decay_row, skip = step_bias[None], decay_log[None], skip_gain[None]
    gain_out_row = gain_out[None]
    w_out_pieces = w_out.T.reshape(pieces, piece, width)
    owners = (mine - jnp.arange(pieces)) % pieces
    w_out_ring = jnp.take(w_out_pieces, owners, axis=0)

    halo = shifted(layer_input[count - EDGE :], "seq", 1)
    halo, grad_columns = tie(halo, output_grad.T)
    cotangents = [grad_columns, turn(grad_columns, "head", 1)]

    whole = lambda *arrays: [(a, "whole") for a in arrays]
    normed, gate, pre, tot, raw, cum, cum_rows, local, payload, fine = call(
        forward_kernel,
        blocks,
        [(layer_input, "rows")]
        + whole(halo, gain_in[None], w_gate, w_inner, w_bc, w_step, conv_inner, conv_bc)
        + whole(conv_inner_bias[None], conv_bc_bias[None], bias_row, decay_row, lower, spread),
        [
            ((count, features), BF16, "rows"),
            ((count, width), F32, "rows"),
            ((count, both), F32, "rows"),
            ((count, both), F32, "rows"),
            ((count, LANES), F32, "rows"),
            ((count, LANES), F32, "rows"),
            ((blocks, 8, BLOCK), F32, "stack"),
            ((blocks, width, states), F32, "stack"),
            ((width + 16, states), BF16, "whole"),
            ((width, states), BF16, "whole"),
        ],
        [(8, both), (width, states), (16, LANES)],
    )
    payload, cotangents[1] = tie(payload, cotangents[1])
    cotangents.append(turn(cotangents[1], "head", 1))
    gathered = lax.all_gather(payload, "seq")
    gathered, fine, cotangents[2] = tie(gathered, fine, cotangents[2])
    incoming = joined_states(gathered, "seq", width, heads, False, lax.all_gather(fine, "seq"))
    for _ in range(pieces - 3):
        cotangents.append(turn(cotangents[-1], "head", 1))
    ssd, starts, squares = call(
        state_kernel,
        blocks,
        [(tot, "rows"), (raw, "rows"), (cum, "rows"), (cum_rows, "stack"), (gate, "rows"), (local, "stack")]
        + whole(incoming, bias_row, skip, hide, spread),
        [
            ((count, width), F32, "rows"),
            ((blocks, width, states), F32, "stack"),
            ((blocks, 8, BLOCK), F32, "stack"),
        ],
        [(width, states)],
    )
    squares, cotangents[-1] = tie(squares, cotangents[-1])
    squares = small_sum(squares, "head")
    dn, cross = call(
        functools.partial(cross_kernel, pieces),
        blocks,
        [(c, "columns") for c in cotangents]
        + whole(w_out_ring)
        + [(ssd, "rows"), (gate, "rows")]
        + whole(gain_out_row),
        [((count, width), F32, "rows"), ((blocks, 8, BLOCK), F32, "stack")],
    )
    cross = small_sum(cross, "head")
    squares_out, dn = tie(squares, dn)
    normed_out, mixed_parts = call(
        functools.partial(out_kernel, all_width),
        blocks,
        [(ssd, "rows"), (gate, "rows"), (squares_out, "stack")] + whole(gain_out_row, w_out_pieces),
        [((count, width), BF16, "rows"), ((pieces, piece, count), BF16, "last")],
    )
    mixed_parts, cross = tie(mixed_parts, cross)
    mixed_ring = ring_scatter(lambda q: lax.dynamic_index_in_dim(mixed_parts, q, 0, False), "head")
    arrived = next(mixed_ring)

    dssd, dgate, local_back, payload_back, gw_out, gw_gate, gate_sums = call(
        functools.partial(gate_kernel, pieces, all_width),
        blocks,
        [(c, "columns") for c in cotangents]
        + [(a, "rows") for a in (ssd, gate, dn, tot, cum, normed, normed_out)]
        + [(squares, "stack"), (cross, "stack")]
        + whole(gain_out_row, spread),
        [
            ((count, width), F32, "rows"),
            ((count, width), BF16, "rows"),
            ((blocks, width, states), F32, "stack"),
            ((width + 16, states), BF16, "whole"),
            ((pieces, piece, width), F32, "whole"),
            ((features, width), F32, "whole"),
            ((8, width), F32, "whole"),
        ],
        [(width, states), (16, LANES)],
        backward=True,
    )
    payload_back, arrived = tie(payload_back, arrived)
    for _ in range(pieces - 3):
        arrived = mixed_ring.send(arrived)
    outgoing = joined_states(lax.all_gather(payload_back, "seq"), "seq", width, heads, True)
    d, draw, rate_sums = call(
        pull_kernel,
        blocks,
        [(tot, "rows"), (raw, "rows"), (cum, "rows"), (cum_rows, "stack"), (dssd, "rows"), (starts, "stack"), (local_back, "stack")]
        + whole(outgoing, bias_row, decay_row, skip, lower, hide, spread),
        [((count, both), F32, "rows"), ((count, LANES), F32, "rows"), ((8, LANES), F32, "whole")],
        [(width, states)],
        backward=True,
    )
    d, arrived = tie(d, arrived)
    arrived = mixed_ring.send(arrived)

    half, half_rows = count // 2, rows // 2
    halo_d = shifted(d[:8], "seq", -1)
    shares, totals = [None, None], []
    for side in (1, 0):
        part, *totals = call(
            functools.partial(project_kernel, len(totals)),
            blocks // 2,
            [(d, "rows")]
            + whole(halo_d)
            + [(pre, "rows"), (normed, "rows"), (dgate, "rows"), (draw, "rows")]
            + whole(gate_sums, rate_sums, conv_inner, conv_bc, w_gate, w_inner, w_bc, w_step, *totals),
            [
                ((half, features), BF16, "rows"),
                ((features, width), F32, "whole"),
                ((features, 2 * states), F32, "whole"),
                ((16, max(features, both)), F32, "whole"),
            ],
            [(8, both)],
            backward=True,
            total=blocks,
            skipped=side * (blocks // 2),
        )
        halo_d = d[half : half + 8]
        if side:
            d, arrived = tie(d, arrived)
        shares[side] = ring_scatter(
            lambda q, part=part: lax.dynamic_slice_in_dim(part, q * half_rows, half_rows, 0), "head"
        )
        running = next(shares[side])
        if side:
            first = running
        else:
            first, part = tie(first, part)
    gw_inner, gw_bc, conv_sums = totals
    gw_out, gw_gate = lax.psum((gw_out, gw_gate), "seq")

    gain_row = gain_in[None]
    runs, blocks_of, sums = {1: first, 0: running}, {}, {}
    for step in range(pieces - 1):
        for side in (1, 0):
            runs[side] = shares[side].send(runs[side])
    runs[1], gw_inner, gw_bc, conv_sums, arrived, layer_late = tie(
        runs[1], gw_inner, gw_bc, conv_sums, arrived, layer_input
    )
    chores = Chores(weight_chores(gw_inner, gw_bc, conv_sums, width))
    for side in (1, 0):
        blocks_of[side], sums[side] = input_call(mine, side, runs[side], layer_input, gain_row, cotangents)
    summed = mixed_ring.send(arrived)
    residual = lax.dynamic_slice_in_dim(layer_late, mine * piece, piece, 1).astype(F32)
    mixed = (residual.T + summed).astype(BF16).T

    arrivals = {side: [blocks_of[side]] for side in (0, 1)}
    for step in range(1, pieces):
        for side in (1, 0):
            blocks_of[side] = turn(blocks_of[side], "head", 1)
            blocks_of[side] = chores.beside(blocks_of[side])
            if step == 1 and side:
                blocks_of[1], gain_part = tie(blocks_of[1], (sums[0] + sums[1])[0].reshape(-1, LANES))
                gains = Chores(gain_chores((gain_part,)))
            else:
                blocks_of[side] = gains.beside(blocks_of[side])
            arrivals[side].append(blocks_of[side])
            if step == pieces - 2 and not side:
                blocks_of[0], gw_out = tie(blocks_of[0], gw_out)
    grad_input = assemble_call(mine, arrivals[0] + arrivals[1])
    gw_inner, gw_bc, sums, bc_sums = chores.finish()
    grad_gain_in = gains.finish()[0].reshape(-1)
    gw_out = jnp.take(gw_out, owners, axis=0).reshape(features, width).T
    head_dim = width // heads
    return (
        mixed,
        grad_input,
        grad_gain_in,
        gw_gate,
        gw_inner,
        gw_bc,
        sums[8 : 8 + heads, :features].T,
        sums[:kernel, :width],
        sums[kernel, :width],
        bc_sums[:kernel],
        bc_sums[kernel],
        sums[kernel + 1, width : width + heads],
        sums[kernel + 2, width : width + heads],
        sums[kernel + 2, :width].reshape(heads, head_dim).sum(1),
        sums[kernel + 1, :width],
        gw_out,
    )


def solution(mesh):
    placed = (
        P("seq", None),
        P(),
        P(None, "head"),
        P(None, "head"),
        P(),
        P(None, "head"),
        P(None, "head"),
        P("head"),
        P(),
        P(),
        P("head"),
        P("head"),
        P("head"),
        P("head"),
        P("head", None),
        P("seq", "head"),
    )
    return jax.shard_map(
        per_device,
        mesh=mesh,
        in_specs=placed,
        out_specs=(
            P("seq", "head"),
            P("seq", None),
            P(),
            P(None, "head"),
            P(None, "head"),
            P(),
            P(None, "head"),
            P(None, "head"),
            P("head"),
            P(),
            P(),
            P("head"),
            P("head"),
            P("head"),
            P("head"),
            P("head", None),
        ),
        check_vma=False,
    )
```

```python
import functools
import jax
import jax.numpy as jnp
import numpy as np
from jax import lax
from jax.experimental import pallas as pl
from jax.experimental.pallas import tpu as pltpu
from jax.sharding import PartitionSpec as P

BLOCK = 256
LANES = 128
EDGE = 16
F32, BF16 = jnp.float32, jnp.bfloat16
eps = 1e-05


def turn(block, axis, distance):
    count = lax.axis_size(axis)
    return lax.ppermute(block, axis, [(i, (i + distance) % count) for i in range(count)])


def shifted(block, axis, distance):
    devices = range(lax.axis_size(axis))
    return lax.ppermute(block, axis, [(i - distance, i) for i in devices if i - distance in devices])


def tie(*values):
    return lax.optimization_barrier(values)


def ring_scatter(parts, axis):
    count, mine = lax.axis_size(axis), lax.axis_index(axis)
    total = parts((mine - 1) % count)
    for step in range(count - 1):
        arrived = yield turn(total, axis, 1)
        total = arrived.astype(F32) + parts((mine - 2 - step) % count).astype(F32)
        if step < count - 2:
            total = total.astype(BF16)
    yield total


def halved(value, axis, reach):
    count, mine = lax.axis_size(axis), lax.axis_index(axis)
    pair = value.reshape(2, value.shape[0] // 2, value.shape[1])
    bit = (mine // reach) % 2
    sent = lax.dynamic_index_in_dim(pair, 1 - bit, 0, False)
    kept = lax.dynamic_index_in_dim(pair, bit, 0, False)
    return kept + lax.ppermute(sent, axis, [(i, i ^ reach) for i in range(count)])


def doubled(value, axis, reach):
    count, mine = lax.axis_size(axis), lax.axis_index(axis)
    other = lax.ppermute(value, axis, [(i, i ^ reach) for i in range(count)])
    second = (mine // reach) % 2 == 1
    return jnp.where(second, jnp.concatenate([other, value], 0), jnp.concatenate([value, other], 0))


def swapped_sum(value, axis, reach):
    return value + lax.ppermute(value, axis, [(i, i ^ reach) for i in range(lax.axis_size(axis))])


def reaches(axis):
    reach, found = 1, []
    while reach < lax.axis_size(axis):
        found.append(reach)
        reach *= 2
    return found


def weight_chores(gw_inner, gw_bc, sums, width):
    for reach in reaches("seq"):
        gw_inner, gw_bc, sums = yield (
            halved(gw_inner, "seq", reach),
            halved(gw_bc, "seq", reach),
            swapped_sum(sums, "seq", reach),
        )
    share = gw_bc.shape[0]
    mine = jnp.concatenate([gw_bc, sums[:8, width : width + gw_bc.shape[1]]], 0)
    shared, gw_inner = yield small_sum(mine, "head"), gw_inner
    gw_bc, bc_sums = shared[:share], shared[share:]
    for reach in reaches("seq")[::-1]:
        gw_inner, gw_bc = yield doubled(gw_inner, "seq", reach), doubled(gw_bc, "seq", reach)
    yield gw_inner, gw_bc, sums, bc_sums


def gain_chores(gain_part):
    gain_part = yield (small_sum(gain_part[0], "head"),)
    for reach in reaches("seq"):
        gain_part = yield (swapped_sum(gain_part[0], "seq", reach),)


class Chores:
    def __init__(self, steps):
        self.steps, self.state = steps, next(steps)

    def beside(self, running):
        if self.steps is not None:
            running, *state = tie(running, *self.state)
            self.advance(tuple(state))
        return running

    def advance(self, state):
        try:
            self.state = self.steps.send(state)
        except StopIteration:
            self.state, self.steps = state, None

    def finish(self):
        while self.steps is not None:
            self.advance(self.state)
        return self.state


def small_sum(value, axis):
    total = value
    for step in range(1, lax.axis_size(axis)):
        total = total + turn(value, axis, step)
    return total


def joined_states(pieces, axis, width, heads, backward, fine=None):
    count, mine = lax.axis_size(axis), lax.axis_index(axis)
    pieces = pieces.astype(F32)
    logs = pieces[:, width, :heads] + pieces[:, width + 8, :heads]
    states = pieces[:, :width]
    if fine is not None:
        states = states + fine.astype(F32)
    place = jnp.arange(count)
    k, m = place[:, None], place[None, :]
    if backward:
        between, counted = (m > mine) & (m < k), place > mine
    else:
        between, counted = (m > k) & (m < mine), place < mine
    passed = jnp.sum(jnp.where(between[:, :, None], logs[None], 0.0), 1)
    weight = jnp.where(counted[:, None], jnp.exp(passed), 0.0)
    weight = jnp.repeat(weight, width // heads, 1)
    return jnp.sum(weight[:, :, None] * states, 0)


def dot(left, right, left_dim=1, right_dim=0, precision=None):
    return lax.dot_general(
        left, right, (((left_dim,), (right_dim,)), ((), ())), precision=precision, preferred_element_type=F32
    )


def silu(value):
    return value * jax.nn.sigmoid(value)


def silu_slope(value):
    s = jax.nn.sigmoid(value)
    return s * (1.0 + value * (1.0 - s))


def halves(value):
    coarse = value.astype(BF16)
    return coarse, (value - coarse.astype(F32)).astype(BF16)


def dot_left(left, right, left_dim=1, right_dim=0):
    coarse, fine = halves(left)
    return dot(coarse, right, left_dim, right_dim) + dot(fine, right, left_dim, right_dim)


def dot_right(left, right, left_dim=1, right_dim=0):
    coarse, fine = halves(right)
    return dot(left, coarse, left_dim, right_dim) + dot(left, fine, left_dim, right_dim)


def dot_both(left, right, left_dim=1, right_dim=0):
    coarse, fine = halves(left)
    return dot_right(coarse, right, left_dim, right_dim) + dot(fine, right.astype(BF16), left_dim, right_dim)


def steps(raw, step_bias):
    moved = raw + step_bias
    return moved, jnp.maximum(moved, 0.0) + jnp.log1p(jnp.exp(-jnp.abs(moved)))


def widen(value, spread):
    return dot_left(value, spread)


def narrow(value, spread):
    return dot_left(value, spread, 1, 1)


def state_decay(last, spread):
    return dot_right(spread, jnp.broadcast_to(jnp.exp(last), (LANES, LANES)).T, 0, 0)


def as_columns(rows, width):
    return dot_left(rows, jnp.full((rows.shape[0], width), 1.0 / rows.shape[0], BF16), 0, 0)


def as_rows(value):
    return dot_right(jnp.ones((8, value.shape[1]), BF16), value, 1, 1)


def row_sum(value):
    return jnp.sum(value, 0, keepdims=True)


def forward_kernel(
    x, halo, gain, w_gate, w_inner, w_bc, w_step, taps_a, taps_b, bias_a, bias_b, step_bias, decay_log, lower, spread,
    normed_o, gate_o, pre_o, tot_o, raw_o, cum_o, cum_rows_o, local_o, payload_o, fine_o,
    before, state, passed,
):
    here, length, width = pl.program_id(0), x.shape[0], w_gate.shape[1]

    def norm(rows):
        rows = rows.astype(F32)
        return (rows * lax.rsqrt(jnp.mean(rows * rows, -1, keepdims=True) + eps) * gain[...]).astype(BF16)

    @pl.when(here == 0)
    def _():
        edge = norm(halo[...])
        before[:, :width] = dot(edge, w_inner[...])[EDGE - 8 :]
        before[:, width:] = dot(edge, w_bc[...])[EDGE - 8 :]
        state[...] = jnp.zeros_like(state)
        passed[...] = jnp.zeros_like(passed)

    normed = norm(x[...])
    normed_o[...] = normed
    gate_o[...] = dot(normed, w_gate[...])
    pre = jnp.concatenate([dot(normed, w_inner[...]), dot(normed, w_bc[...])], 1)
    pre_o[...] = pre
    raw = padded_row(dot(normed, w_step[...]))
    raw_o[...] = raw
    padded = jnp.concatenate([before[...], pre], 0)
    taps = jnp.concatenate([taps_a[...], taps_b[...]], 1)
    kernel = taps.shape[0]
    first = 8 - (kernel - 1)
    total = jnp.concatenate([bias_a[...], bias_b[...]], 1) + sum(taps[k : k + 1, :] * padded[first + k : first + k + length] for k in range(kernel))
    before[...] = pre[length - 8 :]
    tot_o[...] = total
    inner = silu(total[:, :width])
    keys = silu(total[:, width : width + LANES]).astype(BF16)
    _, step = steps(raw, padded_row(step_bias[...]))
    rate = -jnp.exp(padded_row(decay_log[...])) * step
    cum = dot_right(lower[...], rate)
    cum_o[...] = cum
    cum_rows_o[0] = cum.T[:8]
    last = cum[length - 1 : length]
    tail = widen(jnp.exp(last - cum) * step, spread[...])
    local = dot((tail * inner).astype(BF16), keys, 0, 0)
    local_o[0] = local
    state[...] = state_decay(last, spread[...]) * state[...] + local
    passed[...] = passed[...] + last
    write_payload(payload_o, state, passed, fine_o)


def padded_row(row):
    return jnp.concatenate([row, jnp.zeros((row.shape[0], LANES - row.shape[1]), F32)], 1)


def skip_row(skip, spread):
    return widen(jnp.broadcast_to(padded_row(skip[...]), (8, LANES)), spread[...])[0:1]


def write_payload(payload_o, state, passed, fine_o=None):
    width = state.shape[0]

    @pl.when(pl.program_id(0) == pl.num_programs(0) - 1)
    def _():
        payload_o[:width] = state[...].astype(BF16)
        coarse = passed[:8].astype(BF16).astype(F32)
        payload_o[width : width + 16] = jnp.concatenate([coarse, passed[:8] - coarse], 0).astype(BF16)
        if fine_o is not None:
            fine_o[...] = halves(state[...])[1]


def state_kernel(
    tot, raw, cum_in, cum_rows, gate, local, incoming, step_bias, skip, hide, spread,
    ssd_o, start_o, squares_o,
    state,
):
    width = gate.shape[1]

    @pl.when(pl.program_id(0) == 0)
    def _():
        state[...] = incoming[...]

    inner = silu(tot[:, :width])
    keys = silu(tot[:, width : width + LANES]).astype(BF16)
    queries = silu(tot[:, width + LANES :])
    _, step = steps(raw[...], padded_row(step_bias[...]))
    cum = cum_in[...]
    start = state[...]
    start_o[0] = start
    state[...] = state_decay(cum[cum.shape[0] - 1 :], spread[...]) * start + local[0]
    scores = dot_left(queries, keys, 1, 1)
    fed = (inner * widen(step, spread[...])).astype(BF16)
    carried = widen(jnp.exp(cum), spread[...]) * dot_both(queries, start, 1, 1)
    head_dim = width // HEADS_OF(width)
    outs = []
    for begin in range(0, width, LANES):
        size = min(LANES, width - begin)
        pair = fed[:, begin : begin + size]
        lane = lax.broadcasted_iota(jnp.int32, (1, size), 1)
        out = None
        for half in range(size // head_dim):
            h = begin // head_dim + half
            decay = jnp.exp(cum[:, h : h + 1] - cum_rows[0, h : h + 1, :] + hide[...])
            part = dot((scores * decay).astype(BF16), pair)
            out = part if out is None else jnp.where(lane < half * head_dim, out, part)
        outs.append(out)
    ssd = jnp.concatenate(outs, 1) + carried + skip_row(skip, spread) * inner
    ssd_o[...] = ssd
    mixed = ssd * silu(gate[...])
    squares_o[0] = as_rows(mixed * mixed)


HEAD_DIM = 64


def HEADS_OF(width):
    return width // HEAD_DIM


def scale_of(squares, width, all_width):
    return lax.rsqrt(as_columns(squares, width) / all_width + eps)


def out_kernel(all_width, ssd, gate, squares, gain, w_out, normed_o, part_o):
    width = ssd.shape[1]
    mixed = ssd[...] * silu(gate[...])
    normed = (mixed * scale_of(squares[0], width, all_width) * gain[...]).astype(BF16)
    normed_o[...] = normed
    for piece in range(w_out.shape[0]):
        part_o[piece] = dot(w_out[piece], normed, 1, 1).astype(BF16)


def cross_kernel(pieces, *refs):
    grads, (w_out, ssd, gate, gain, dn_o, cross_o) = refs[:pieces], refs[pieces:]
    dn = sum(dot(grads[p][...], w_out[p], 0, 0) for p in range(pieces))
    dn_o[...] = dn
    cross_o[0] = as_rows(dn * gain[...] * (ssd[...] * silu(gate[...])))


def gate_kernel(pieces, all_width, *refs):
    grads = refs[:pieces]
    (
        ssd, gate, dn, tot, cum_in, normed, normed_out, squares, cross, gain, spread,
        dssd_o, dgate_o, local_o, payload_o, fine_o, gw_out_o, gw_gate_o, sums_o,
        state, passed,
    ) = refs[pieces:]
    width, length = ssd.shape[1], ssd.shape[0]

    @pl.when(pl.program_id(0) == 0)
    def _():
        state[...] = jnp.zeros_like(state)
        passed[...] = jnp.zeros_like(passed)
        gw_out_o[...] = jnp.zeros_like(gw_out_o)
        gw_gate_o[...] = jnp.zeros_like(gw_gate_o)
        sums_o[...] = jnp.zeros_like(sums_o)

    g = gate[...]
    s = jax.nn.sigmoid(g)
    act = g * s
    mixed = ssd[...] * act
    scale = scale_of(squares[0], width, all_width)
    dscaled = dn[...] * scale
    along = as_columns(cross[0] / (squares[0] + all_width * eps), width)
    dmixed = scale * (dn[...] * gain[...] - mixed * along)
    dssd = dmixed * act
    dssd_o[...] = dssd
    dgate = (dmixed * ssd[...] * s * (1.0 + g * (1.0 - s))).astype(BF16)
    dgate_o[...] = dgate
    inner = silu(tot[:, :width])
    queries = silu(tot[:, width + LANES :])
    sums_o[0:1] = sums_o[0:1] + row_sum(dscaled * mixed)
    sums_o[1:2] = sums_o[1:2] + row_sum(dssd * inner)
    cum = cum_in[...]
    local = dot_both(widen(jnp.exp(cum), spread[...]) * dssd, queries, 0, 0)
    local_o[0] = local
    state[...] = state_decay(cum[length - 1 :], spread[...]) * state[...] + local
    passed[...] = passed[...] + cum[length - 1 :]
    for p in range(pieces):
        gw_out_o[p] = gw_out_o[p] + dot(grads[p][...], normed_out[...])
    gw_gate_o[...] = gw_gate_o[...] + dot(normed[...], dgate, 0, 0)
    write_payload(payload_o, state, passed, fine_o)


def pull_kernel(
    tot, raw, cum_in, cum_rows, dssd, start, local, outgoing, step_bias, decay_log, skip, lower, hide, spread,
    d_o, draw_o, sums_o,
    state,
):
    width, length = dssd.shape[1], dssd.shape[0]

    @pl.when(pl.program_id(0) == 0)
    def _():
        state[...] = outgoing[...]
        sums_o[...] = jnp.zeros_like(sums_o)

    inner = silu(tot[:, :width])
    keys = silu(tot[:, width : width + LANES]).astype(BF16)
    queries = silu(tot[:, width + LANES :])
    shifted_raw, step = steps(raw[...], padded_row(step_bias[...]))
    growth = jnp.exp(padded_row(decay_log[...]))
    rate = -growth * step
    cum = cum_in[...]
    last = cum[length - 1 : length]
    ending = state[...]
    state[...] = state_decay(last, spread[...]) * ending + local[0]
    beginning = start[0]
    dy = dssd[...]
    dy16, dy_fine = halves(dy)
    ecum = jnp.exp(cum)
    tail = jnp.exp(last - cum)
    step_w = widen(step, spread[...])
    ecum_w = widen(ecum, spread[...])
    tail_w = widen(tail * step, spread[...])
    read = dot(queries.astype(BF16), beginning.astype(BF16), 1, 1)
    dqueries = dot_both(ecum_w * dy, beginning)
    taken = dot(keys, ending.astype(BF16), 1, 1)
    dkeys = dot_both(tail_w * inner, ending)
    from_start = ecum * narrow(dy * read, spread[...])
    to_end = tail * narrow(inner * taken, spread[...])
    both = as_rows(ending * beginning)
    through = jnp.exp(last) * narrow(both, spread[...])[0:1]
    scores = dot_left(queries, keys, 1, 1)
    fed, fed_fine = halves(inner * step_w)
    dscores = jnp.zeros_like(scores)
    crossing = jnp.zeros((length, LANES), F32)
    pulls, downs = [], []
    lanes_all = lax.broadcasted_iota(jnp.int32, (length, LANES), 1)
    for begin in range(0, width, LANES):
        size = min(LANES, width - begin)
        fed_pair, fed_low, dy_pair, dy_low = (v[:, begin : begin + size] for v in (fed, fed_fine, dy16, dy_fine))
        lane = lax.broadcasted_iota(jnp.int32, (1, size), 1)
        rows = []
        for half in range(size // HEAD_DIM):
            h = begin // HEAD_DIM + half
            inside = (lane >= half * HEAD_DIM) & (lane < (half + 1) * HEAD_DIM)
            fed_head = jnp.where(inside, fed_pair, jnp.zeros_like(fed_pair))
            low_head = jnp.where(inside, fed_low, jnp.zeros_like(fed_low))
            decay = jnp.exp(cum[:, h : h + 1] - cum_rows[0, h : h + 1, :] + hide[...])
            dweight = dot(dy_pair, fed_head, 1, 1) + dot(dy_low, fed_head, 1, 1) + dot(dy_pair, low_head, 1, 1)
            dweight = dweight * decay
            dscores = dscores + dweight
            weight = (scores * decay).astype(BF16)
            pulled = dot(dy_pair, weight, 0, 0)
            rows.append(pulled[half * HEAD_DIM : (half + 1) * HEAD_DIM])
            pair_terms = dweight * scores
            right = jnp.sum(pair_terms, 1, keepdims=True)
            downs.append(jnp.sum(pair_terms, 0, keepdims=True))
            crossing = jnp.where(lanes_all == h, right, crossing)
        pulls.append(jnp.concatenate(rows, 0).T)
    pulled = jnp.concatenate(pulls, 1)
    downs.append(jnp.zeros((LANES - len(downs), length), F32))
    crossing = crossing - jnp.concatenate(downs, 0).T
    coarse, fine = halves(dscores)
    dqueries = dqueries + dot(coarse, keys) + dot(fine, keys)
    dkeys = dkeys + (dot_left(queries, coarse, 0, 0) + dot(queries.astype(BF16), fine, 0, 0)).T
    dinner = (tail_w * taken + step_w * pulled) + skip_row(skip, spread) * dy
    dstep = narrow(inner * pulled, spread[...]) + to_end
    given = to_end * step
    drate = dot_right(lower[...], crossing + from_start, 0, 0) + (dot_right(lower[...], given) - given)
    drate = drate + through
    dstep = dstep - growth * drate
    draw = dstep * jax.nn.sigmoid(shifted_raw)
    draw_o[...] = draw
    sums_o[0:1] = sums_o[0:1] + row_sum(draw)
    sums_o[1:2] = sums_o[1:2] + row_sum(rate * drate)
    d_o[:, :width] = dinner * silu_slope(tot[:, :width])
    d_o[:, width : width + LANES] = dkeys * silu_slope(tot[:, width : width + LANES])
    d_o[:, width + LANES :] = dqueries * silu_slope(tot[:, width + LANES :])


def project_kernel(
    earlier, d, halo, pre, normed, dgate, draw, gate_sums, rate_sums, taps_a, taps_b, w_gate, w_inner, w_bc, w_step, *refs
):
    given, (part_o, *totals, after) = refs[:earlier], refs[earlier:]
    gw_inner_o, gw_bc_o, sums_o = totals
    width, length = w_gate.shape[1], d.shape[0]

    @pl.when(pl.program_id(0) == 0)
    def _():
        after[...] = halo[...]
        for at, out in enumerate(totals):
            out[...] = given[at][...] if earlier else jnp.zeros_like(out)
        if not earlier:
            rows = jnp.concatenate([gate_sums[0:2], rate_sums[0:2], jnp.zeros((2, LANES), F32)], 1)
            sums_o[taps_a.shape[0] + 1 : taps_a.shape[0] + 3, : rows.shape[1]] = rows

    taps = jnp.concatenate([taps_a[...], taps_b[...]], 1)
    kernel, heads, both = taps.shape[0], w_step.shape[1], taps.shape[1]
    features = normed.shape[1]
    grads = d[...]
    padded = jnp.concatenate([grads, after[...]], 0)
    after[...] = grads[:8]
    dpre = jnp.zeros_like(grads)
    for k in range(kernel):
        moved = padded[kernel - 1 - k : kernel - 1 - k + length]
        dpre = dpre + taps[k : k + 1, :] * moved
        sums_o[k : k + 1, :both] = sums_o[k : k + 1, :both] + row_sum(pre[...] * moved)
    sums_o[kernel : kernel + 1, :both] = sums_o[kernel : kernel + 1, :both] + row_sum(grads)
    dinner, dbc, dstep = dpre[:, :width].astype(BF16), dpre[:, width:], draw[:, :heads].astype(BF16)
    part = dot(dgate[...], w_gate[...], 1, 1) + dot(dinner, w_inner[...], 1, 1)
    part = part + dot_left(dbc, w_bc[...], 1, 1) + dot(dstep, w_step[...], 1, 1)
    part_o[...] = part.astype(BF16)
    gw_inner_o[...] = gw_inner_o[...] + dot(normed[...], dinner, 0, 0)
    gw_bc_o[...] = gw_bc_o[...] + dot_right(normed[...], dbc, 0, 0)
    sums_o[8 : 8 + heads, :features] = sums_o[8 : 8 + heads, :features] + dot(dstep, normed[...], 0, 0)


def input_kernel(place, dnormed, x, gain, *refs):
    pieces = len(refs) - 3
    grads, (block_o, sums_o, columns) = refs[:pieces], refs[pieces:]
    for p in range(pieces):
        columns[(place[0] - p + pieces) % pieces] = grads[p][...].astype(F32)
    cotangent = jnp.concatenate([columns[q] for q in range(pieces)], 0).T
    rows = x[...].astype(F32)
    scale = lax.rsqrt(jnp.mean(rows * rows, -1, keepdims=True) + eps)
    scaled = dnormed[...] * gain[...]
    sums_o[...] = jnp.broadcast_to(row_sum(dnormed[...] * rows * scale), sums_o.shape)
    along = rows * (scale * scale * scale * jnp.mean(scaled * rows, -1, keepdims=True))
    block_o[...] = (scaled * scale - along + cotangent).astype(BF16)


def input_call(mine, side, dnormed, layer_input, gain, cotangents):
    rows, features = dnormed.shape
    pieces = len(cotangents)
    piece = cotangents[0].shape[0]
    return pl.pallas_call(
        input_kernel,
        grid_spec=pltpu.PrefetchScalarGridSpec(
            num_scalar_prefetch=1,
            grid=(1,),
            in_specs=[
                pl.BlockSpec((rows, features), lambda i, place: (0, 0)),
                pl.BlockSpec((rows, features), lambda i, place: (side * pieces + place[0], 0)),
                pl.BlockSpec((1, features), lambda i, place: (0, 0)),
            ]
            + [pl.BlockSpec((piece, rows), lambda i, place: (0, side * pieces + place[0]))] * pieces,
            out_specs=[
                pl.BlockSpec((rows, features), lambda i, place: (0, 0)),
                pl.BlockSpec((8, features), lambda i, place: (0, 0)),
            ],
            scratch_shapes=[pltpu.VMEM((pieces, piece, rows), F32)],
        ),
        out_shape=[jax.ShapeDtypeStruct((rows, features), BF16), jax.ShapeDtypeStruct((8, features), F32)],
        compiler_params=pltpu.CompilerParams(
            dimension_semantics=("arbitrary",), vmem_limit_bytes=60 * 1024 * 1024
        ),
        cost_estimate=pl.CostEstimate(flops=10**6, bytes_accessed=10**4, transcendentals=0),
    )(mine[None].astype(jnp.int32), dnormed, layer_input, gain, *cotangents)


def assemble_kernel(given, place, *refs):
    blocks, out = refs[given:-1], refs[-1]
    wanted = (place[0] - pl.program_id(0) + len(blocks)) % len(blocks)
    for at, block in enumerate(blocks):

        @pl.when(wanted == at)
        def _():
            out[...] = block[...].astype(F32)


def assemble_call(mine, side, blocks, total, given=()):
    rows, features = blocks[0].shape
    pieces = len(blocks)
    return pl.pallas_call(
        functools.partial(assemble_kernel, len(given)),
        grid_spec=pltpu.PrefetchScalarGridSpec(
            num_scalar_prefetch=1,
            grid=(pieces,),
            in_specs=[pl.BlockSpec(memory_space=pl.ANY)] * len(given)
            + [pl.BlockSpec((rows, features), lambda i, place: (0, 0))] * pieces,
            out_specs=pl.BlockSpec((rows, features), lambda i, place: (side * pieces + i, 0)),
        ),
        out_shape=jax.ShapeDtypeStruct((total, features), F32),
        input_output_aliases={1: 0} if given else {},
        compiler_params=pltpu.CompilerParams(
            dimension_semantics=("arbitrary",), vmem_limit_bytes=60 * 1024 * 1024
        ),
        cost_estimate=pl.CostEstimate(flops=10**6, bytes_accessed=10**4, transcendentals=0),
    )(mine[None].astype(jnp.int32), *given, *blocks)


def call(kernel, blocks, ins, outs, scratch=(), backward=False, total=None, skipped=0):
    steps_here = blocks

    def spec(shape, kind, blocks=blocks, skipped=0):
        def at(i):
            return skipped + (steps_here - 1 - i if backward else i)

        if kind == "rows":
            return pl.BlockSpec((shape[0] // blocks,) + shape[1:], lambda i: (at(i), 0))
        if kind == "stack":
            return pl.BlockSpec((1,) + shape[1:], lambda i: (at(i), 0, 0))
        if kind == "columns":
            return pl.BlockSpec((shape[0], shape[1] // blocks), lambda i: (0, at(i)))
        if kind == "last":
            return pl.BlockSpec((shape[0], shape[1], shape[2] // blocks), lambda i: (0, 0, at(i)))
        return pl.BlockSpec(shape, lambda i: (0,) * len(shape))

    return pl.pallas_call(
        kernel,
        grid=(blocks,),
        in_specs=[spec(a.shape, kind, total or blocks, skipped) for a, kind in ins],
        out_specs=[spec(shape, kind) for shape, _, kind in outs],
        out_shape=[jax.ShapeDtypeStruct(shape, dtype) for shape, dtype, _ in outs],
        scratch_shapes=[pltpu.VMEM(shape, F32) for shape in scratch],
        compiler_params=pltpu.CompilerParams(
            dimension_semantics=("arbitrary",), vmem_limit_bytes=60 * 1024 * 1024
        ),
        cost_estimate=pl.CostEstimate(flops=10**6, bytes_accessed=10**4, transcendentals=0),
    )(*[a for a, _ in ins])


def per_device(
    layer_input, gain_in, w_gate, w_inner, w_bc, w_step, conv_inner, conv_inner_bias, conv_bc, conv_bc_bias,
    step_bias, decay_log, skip_gain, gain_out, w_out, output_grad,
):
    count, features = layer_input.shape
    heads, width = decay_log.shape[0], w_gate.shape[1]
    states = w_bc.shape[1] // 2
    both = width + 2 * states
    blocks = count // BLOCK
    kernel = conv_inner.shape[0]
    pieces, mine = lax.axis_size("head"), lax.axis_index("head")
    all_width = width * pieces
    piece = output_grad.shape[1]
    rows = count // pieces

    place = np.arange(BLOCK)
    keep = place[:, None] >= place[None, :]
    lower = jnp.asarray(keep, BF16)
    hide = jnp.asarray(np.where(keep, 0.0, -1e30), F32)
    spread = jnp.asarray(np.arange(LANES)[:, None] == (np.arange(width) // (width // heads))[None, :], BF16)
    bias_row, decay_row, skip = step_bias[None], decay_log[None], skip_gain[None]
    gain_out_row = gain_out[None]
    w_out_pieces = w_out.T.reshape(pieces, piece, width)
    owners = (mine - jnp.arange(pieces)) % pieces
    w_out_ring = jnp.take(w_out_pieces, owners, axis=0)

    halo = shifted(layer_input[count - EDGE :], "seq", 1)
    halo, grad_columns = tie(halo, output_grad.T)
    cotangents = [grad_columns, turn(grad_columns, "head", 1)]

    whole = lambda *arrays: [(a, "whole") for a in arrays]
    normed, gate, pre, tot, raw, cum, cum_rows, local, payload, fine = call(
        forward_kernel,
        blocks,
        [(layer_input, "rows")]
        + whole(halo, gain_in[None], w_gate, w_inner, w_bc, w_step, conv_inner, conv_bc)
        + whole(conv_inner_bias[None], conv_bc_bias[None], bias_row, decay_row, lower, spread),
        [
            ((count, features), BF16, "rows"),
            ((count, width), F32, "rows"),
            ((count, both), F32, "rows"),
            ((count, both), F32, "rows"),
            ((count, LANES), F32, "rows"),
            ((count, LANES), F32, "rows"),
            ((blocks, 8, BLOCK), F32, "stack"),
            ((blocks, width, states), F32, "stack"),
            ((width + 16, states), BF16, "whole"),
            ((width, states), BF16, "whole"),
        ],
        [(8, both), (width, states), (16, LANES)],
    )
    payload, cotangents[1] = tie(payload, cotangents[1])
    cotangents.append(turn(cotangents[1], "head", 1))
    gathered = lax.all_gather(payload, "seq")
    gathered, fine, cotangents[2] = tie(gathered, fine, cotangents[2])
    incoming = joined_states(gathered, "seq", width, heads, False, lax.all_gather(fine, "seq"))
    for _ in range(pieces - 3):
        cotangents.append(turn(cotangents[-1], "head", 1))
    ssd, starts, squares = call(
        state_kernel,
        blocks,
        [(tot, "rows"), (raw, "rows"), (cum, "rows"), (cum_rows, "stack"), (gate, "rows"), (local, "stack")]
        + whole(incoming, bias_row, skip, hide, spread),
        [
            ((count, width), F32, "rows"),
            ((blocks, width, states), F32, "stack"),
            ((blocks, 8, BLOCK), F32, "stack"),
        ],
        [(width, states)],
    )
    squares, cotangents[-1] = tie(squares, cotangents[-1])
    squares = small_sum(squares, "head")
    dn, cross = call(
        functools.partial(cross_kernel, pieces),
        blocks,
        [(c, "columns") for c in cotangents]
        + whole(w_out_ring)
        + [(ssd, "rows"), (gate, "rows")]
        + whole(gain_out_row),
        [((count, width), F32, "rows"), ((blocks, 8, BLOCK), F32, "stack")],
    )
    cross = small_sum(cross, "head")
    squares_out, dn = tie(squares, dn)
    normed_out, mixed_parts = call(
        functools.partial(out_kernel, all_width),
        blocks,
        [(ssd, "rows"), (gate, "rows"), (squares_out, "stack")] + whole(gain_out_row, w_out_pieces),
        [((count, width), BF16, "rows"), ((pieces, piece, count), BF16, "last")],
    )
    mixed_parts, cross = tie(mixed_parts, cross)
    mixed_ring = ring_scatter(lambda q: lax.dynamic_index_in_dim(mixed_parts, q, 0, False), "head")
    arrived = next(mixed_ring)

    dssd, dgate, local_back, payload_back, fine_back, gw_out, gw_gate, gate_sums = call(
        functools.partial(gate_kernel, pieces, all_width),
        blocks,
        [(c, "columns") for c in cotangents]
        + [(a, "rows") for a in (ssd, gate, dn, tot, cum, normed, normed_out)]
        + [(squares, "stack"), (cross, "stack")]
        + whole(gain_out_row, spread),
        [
            ((count, width), F32, "rows"),
            ((count, width), BF16, "rows"),
            ((blocks, width, states), F32, "stack"),
            ((width + 16, states), BF16, "whole"),
            ((width, states), BF16, "whole"),
            ((pieces, piece, width), F32, "whole"),
            ((features, width), F32, "whole"),
            ((8, width), F32, "whole"),
        ],
        [(width, states), (16, LANES)],
        backward=True,
    )
    payload_back, arrived = tie(payload_back, arrived)
    gathered_back = lax.all_gather(payload_back, "seq")
    for _ in range(pieces - 3):
        arrived = mixed_ring.send(arrived)
    outgoing = joined_states(gathered_back, "seq", width, heads, True, lax.all_gather(fine_back, "seq"))
    d, draw, rate_sums = call(
        pull_kernel,
        blocks,
        [(tot, "rows"), (raw, "rows"), (cum, "rows"), (cum_rows, "stack"), (dssd, "rows"), (starts, "stack"), (local_back, "stack")]
        + whole(outgoing, bias_row, decay_row, skip, lower, hide, spread),
        [((count, both), F32, "rows"), ((count, LANES), F32, "rows"), ((8, LANES), F32, "whole")],
        [(width, states)],
        backward=True,
    )
    d, arrived = tie(d, arrived)
    arrived = mixed_ring.send(arrived)

    half, half_rows = count // 2, rows // 2
    halo_d = shifted(d[:8], "seq", -1)
    shares, totals = [None, None], []
    for side in (1, 0):
        part, *totals = call(
            functools.partial(project_kernel, len(totals)),
            blocks // 2,
            [(d, "rows")]
            + whole(halo_d)
            + [(pre, "rows"), (normed, "rows"), (dgate, "rows"), (draw, "rows")]
            + whole(gate_sums, rate_sums, conv_inner, conv_bc, w_gate, w_inner, w_bc, w_step, *totals),
            [
                ((half, features), BF16, "rows"),
                ((features, width), F32, "whole"),
                ((features, 2 * states), F32, "whole"),
                ((16, max(features, both)), F32, "whole"),
            ],
            [(8, both)],
            backward=True,
            total=blocks,
            skipped=side * (blocks // 2),
        )
        halo_d = d[half : half + 8]
        if side:
            d, arrived, gw_out, gw_gate = tie(d, arrived, *lax.psum((gw_out, gw_gate), "seq"))
        shares[side] = ring_scatter(
            lambda q, part=part: lax.dynamic_slice_in_dim(part, q * half_rows, half_rows, 0), "head"
        )
        running = next(shares[side])
        if side:
            first = running
        else:
            first, part = tie(first, part)
    gw_inner, gw_bc, conv_sums = totals

    gain_row = gain_in[None]
    runs, blocks_of, sums = {1: first, 0: running}, {}, {}
    runs[1], gw_inner, gw_bc, conv_sums = tie(runs[1], gw_inner, gw_bc, conv_sums)
    chores = Chores(weight_chores(gw_inner, gw_bc, conv_sums, width))
    for step in range(pieces - 1):
        for side in (1, 0):
            runs[side] = shares[side].send(runs[side])
            if side and step < pieces - 2:
                runs[1] = chores.beside(runs[1])
    runs[0], arrived, layer_late = tie(runs[0], arrived, layer_input)
    for side in (1, 0):
        blocks_of[side], sums[side] = input_call(mine, side, runs[side], layer_input, gain_row, cotangents)
    summed = mixed_ring.send(arrived)
    residual = lax.dynamic_slice_in_dim(layer_late, mine * piece, piece, 1).astype(F32)
    mixed = (residual.T + summed).astype(BF16).T

    arrivals = {side: [blocks_of[side]] for side in (0, 1)}
    for step in range(1, pieces):
        for side in (1, 0):
            blocks_of[side] = turn(blocks_of[side], "head", 1)
            if step > 1 or side:
                blocks_of[side] = chores.beside(blocks_of[side])
            if step == 1 and side:
                blocks_of[1], gain_part = tie(blocks_of[1], (sums[0] + sums[1])[0].reshape(-1, LANES))
                gains = Chores(gain_chores((gain_part,)))
            elif step > 1:
                blocks_of[side] = gains.beside(blocks_of[side])
            arrivals[side].append(blocks_of[side])
            if step == 1 and not side:
                blocks_of[0], gw_out = tie(blocks_of[0], gw_out)
    grad_input = assemble_call(mine, 1, arrivals[1], count)
    grad_input = assemble_call(mine, 0, arrivals[0], count, (grad_input,))
    gw_inner, gw_bc, sums, bc_sums = chores.finish()
    grad_gain_in = gains.finish()[0].reshape(-1)
    gw_out = jnp.take(gw_out, owners, axis=0).reshape(features, width).T
    head_dim = width // heads
    return (
        mixed,
        grad_input,
        grad_gain_in,
        gw_gate,
        gw_inner,
        gw_bc,
        sums[8 : 8 + heads, :features].T,
        sums[:kernel, :width],
        sums[kernel, :width],
        bc_sums[:kernel],
        bc_sums[kernel],
        sums[kernel + 1, width : width + heads],
        sums[kernel + 2, width : width + heads],
        sums[kernel + 2, :width].reshape(heads, head_dim).sum(1),
        sums[kernel + 1, :width],
        gw_out,
    )


def solution(mesh):
    placed = (
        P("seq", None),
        P(),
        P(None, "head"),
        P(None, "head"),
        P(),
        P(None, "head"),
        P(None, "head"),
        P("head"),
        P(),
        P(),
        P("head"),
        P("head"),
        P("head"),
        P("head"),
        P("head", None),
        P("seq", "head"),
    )
    return jax.shard_map(
        per_device,
        mesh=mesh,
        in_specs=placed,
        out_specs=(
            P("seq", "head"),
            P("seq", None),
            P(),
            P(None, "head"),
            P(None, "head"),
            P(),
            P(None, "head"),
            P(None, "head"),
            P("head"),
            P(),
            P(),
            P("head"),
            P("head"),
            P("head"),
            P("head"),
            P("head", None),
        ),
        check_vma=False,
    )
```

```python
import functools
import jax
import jax.numpy as jnp
import numpy as np
from jax import lax
from jax.experimental import pallas as pl
from jax.experimental.pallas import tpu as pltpu
from jax.sharding import PartitionSpec as P

BLOCK = 256
LANES = 128
EDGE = 16
F32, BF16 = jnp.float32, jnp.bfloat16
eps = 1e-05


def turn(block, axis, distance):
    count = lax.axis_size(axis)
    return lax.ppermute(block, axis, [(i, (i + distance) % count) for i in range(count)])


def shifted(block, axis, distance):
    devices = range(lax.axis_size(axis))
    return lax.ppermute(block, axis, [(i - distance, i) for i in devices if i - distance in devices])


def tie(*values):
    return lax.optimization_barrier(values)


def ring_scatter(parts, axis):
    count, mine = lax.axis_size(axis), lax.axis_index(axis)
    total = parts((mine - 1) % count)
    for step in range(count - 1):
        arrived = yield turn(total, axis, 1)
        total = arrived.astype(F32) + parts((mine - 2 - step) % count).astype(F32)
        if step < count - 2:
            total = total.astype(BF16)
    yield total


def halved(value, axis, reach):
    count, mine = lax.axis_size(axis), lax.axis_index(axis)
    pair = value.reshape(2, value.shape[0] // 2, value.shape[1])
    bit = (mine // reach) % 2
    sent = lax.dynamic_index_in_dim(pair, 1 - bit, 0, False)
    kept = lax.dynamic_index_in_dim(pair, bit, 0, False)
    return kept + lax.ppermute(sent, axis, [(i, i ^ reach) for i in range(count)])


def doubled(value, axis, reach):
    count, mine = lax.axis_size(axis), lax.axis_index(axis)
    other = lax.ppermute(value, axis, [(i, i ^ reach) for i in range(count)])
    second = (mine // reach) % 2 == 1
    return jnp.where(second, jnp.concatenate([other, value], 0), jnp.concatenate([value, other], 0))


def swapped_sum(value, axis, reach):
    return value + lax.ppermute(value, axis, [(i, i ^ reach) for i in range(lax.axis_size(axis))])


def reaches(axis):
    reach, found = 1, []
    while reach < lax.axis_size(axis):
        found.append(reach)
        reach *= 2
    return found


def weight_chores(gw_inner, gw_bc, sums, width):
    for reach in reaches("seq"):
        gw_inner, gw_bc, sums = yield (
            halved(gw_inner, "seq", reach),
            halved(gw_bc, "seq", reach),
            swapped_sum(sums, "seq", reach),
        )
    share = gw_bc.shape[0]
    mine = jnp.concatenate([gw_bc, sums[:8, width : width + gw_bc.shape[1]]], 0)
    shared, gw_inner = yield small_sum(mine, "head"), gw_inner
    gw_bc, bc_sums = shared[:share], shared[share:]
    for reach in reaches("seq")[::-1]:
        gw_inner, gw_bc = yield doubled(gw_inner, "seq", reach), doubled(gw_bc, "seq", reach)
    yield gw_inner, gw_bc, sums, bc_sums


def gain_chores(gain_part):
    gain_part = yield (small_sum(gain_part[0], "head"),)
    for reach in reaches("seq"):
        gain_part = yield (swapped_sum(gain_part[0], "seq", reach),)


class Chores:
    def __init__(self, steps):
        self.steps, self.state = steps, next(steps)

    def beside(self, running):
        if self.steps is not None:
            running, *state = tie(running, *self.state)
            self.advance(tuple(state))
        return running

    def advance(self, state):
        try:
            self.state = self.steps.send(state)
        except StopIteration:
            self.state, self.steps = state, None

    def finish(self):
        while self.steps is not None:
            self.advance(self.state)
        return self.state


def small_sum(value, axis):
    total = value
    for step in range(1, lax.axis_size(axis)):
        total = total + turn(value, axis, step)
    return total


def joined_states(pieces, axis, width, heads, backward, fine=None):
    count, mine = lax.axis_size(axis), lax.axis_index(axis)
    pieces = pieces.astype(F32)
    logs = pieces[:, width, :heads] + pieces[:, width + 8, :heads]
    states = pieces[:, :width]
    if fine is not None:
        states = states + fine.astype(F32)
    place = jnp.arange(count)
    k, m = place[:, None], place[None, :]
    if backward:
        between, counted = (m > mine) & (m < k), place > mine
    else:
        between, counted = (m > k) & (m < mine), place < mine
    passed = jnp.sum(jnp.where(between[:, :, None], logs[None], 0.0), 1)
    weight = jnp.where(counted[:, None], jnp.exp(passed), 0.0)
    weight = jnp.repeat(weight, width // heads, 1)
    return jnp.sum(weight[:, :, None] * states, 0)


def dot(left, right, left_dim=1, right_dim=0, precision=None):
    return lax.dot_general(
        left, right, (((left_dim,), (right_dim,)), ((), ())), precision=precision, preferred_element_type=F32
    )


def silu(value):
    return value * jax.nn.sigmoid(value)


def silu_slope(value):
    s = jax.nn.sigmoid(value)
    return s * (1.0 + value * (1.0 - s))


def halves(value):
    coarse = value.astype(BF16)
    return coarse, (value - coarse.astype(F32)).astype(BF16)


def dot_left(left, right, left_dim=1, right_dim=0):
    coarse, fine = halves(left)
    return dot(coarse, right, left_dim, right_dim) + dot(fine, right, left_dim, right_dim)


def dot_right(left, right, left_dim=1, right_dim=0):
    coarse, fine = halves(right)
    return dot(left, coarse, left_dim, right_dim) + dot(left, fine, left_dim, right_dim)


def dot_both(left, right, left_dim=1, right_dim=0):
    coarse, fine = halves(left)
    return dot_right(coarse, right, left_dim, right_dim) + dot(fine, right.astype(BF16), left_dim, right_dim)


def steps(raw, step_bias):
    moved = raw + step_bias
    return moved, jnp.maximum(moved, 0.0) + jnp.log1p(jnp.exp(-jnp.abs(moved)))


def widen(value, spread):
    return dot_left(value, spread)


def narrow(value, spread):
    return dot_left(value, spread, 1, 1)


def state_decay(last, spread):
    return dot_right(spread, jnp.broadcast_to(jnp.exp(last), (LANES, LANES)).T, 0, 0)


def as_columns(rows, width):
    return dot_left(rows, jnp.full((rows.shape[0], width), 1.0 / rows.shape[0], BF16), 0, 0)


def as_rows(value):
    return dot_right(jnp.ones((8, value.shape[1]), BF16), value, 1, 1)


def row_sum(value):
    return jnp.sum(value, 0, keepdims=True)


def forward_kernel(
    x, halo, gain, w_gate, w_inner, w_bc, w_step, taps_a, taps_b, bias_a, bias_b, step_bias, decay_log, lower, spread,
    normed_o, gate_o, pre_o, tot_o, raw_o, cum_o, cum_rows_o, local_o, payload_o, fine_o,
    before, state, passed,
):
    here, length, width = pl.program_id(0), x.shape[0], w_gate.shape[1]

    def norm(rows):
        rows = rows.astype(F32)
        return (rows * lax.rsqrt(jnp.mean(rows * rows, -1, keepdims=True) + eps) * gain[...]).astype(BF16)

    @pl.when(here == 0)
    def _():
        edge = norm(halo[...])
        before[:, :width] = dot(edge, w_inner[...])[EDGE - 8 :]
        before[:, width:] = dot(edge, w_bc[...])[EDGE - 8 :]
        state[...] = jnp.zeros_like(state)
        passed[...] = jnp.zeros_like(passed)

    normed = norm(x[...])
    normed_o[...] = normed
    gate_o[...] = dot(normed, w_gate[...])
    pre = jnp.concatenate([dot(normed, w_inner[...]), dot(normed, w_bc[...])], 1)
    pre_o[...] = pre
    raw = padded_row(dot(normed, w_step[...]))
    raw_o[...] = raw
    padded = jnp.concatenate([before[...], pre], 0)
    taps = jnp.concatenate([taps_a[...], taps_b[...]], 1)
    kernel = taps.shape[0]
    first = 8 - (kernel - 1)
    total = jnp.concatenate([bias_a[...], bias_b[...]], 1) + sum(taps[k : k + 1, :] * padded[first + k : first + k + length] for k in range(kernel))
    before[...] = pre[length - 8 :]
    tot_o[...] = total
    inner = silu(total[:, :width])
    keys = silu(total[:, width : width + LANES]).astype(BF16)
    _, step = steps(raw, padded_row(step_bias[...]))
    rate = -jnp.exp(padded_row(decay_log[...])) * step
    cum = dot_right(lower[...], rate)
    cum_o[...] = cum
    cum_rows_o[0] = cum.T[:8]
    last = cum[length - 1 : length]
    tail = widen(jnp.exp(last - cum) * step, spread[...])
    local = dot((tail * inner).astype(BF16), keys, 0, 0)
    local_o[0] = local
    state[...] = state_decay(last, spread[...]) * state[...] + local
    passed[...] = passed[...] + last
    write_payload(payload_o, state, passed, fine_o)


def padded_row(row):
    return jnp.concatenate([row, jnp.zeros((row.shape[0], LANES - row.shape[1]), F32)], 1)


def skip_row(skip, spread):
    return widen(jnp.broadcast_to(padded_row(skip[...]), (8, LANES)), spread[...])[0:1]


def write_payload(payload_o, state, passed, fine_o=None):
    width = state.shape[0]

    @pl.when(pl.program_id(0) == pl.num_programs(0) - 1)
    def _():
        payload_o[:width] = state[...].astype(BF16)
        coarse = passed[:8].astype(BF16).astype(F32)
        payload_o[width : width + 16] = jnp.concatenate([coarse, passed[:8] - coarse], 0).astype(BF16)
        if fine_o is not None:
            fine_o[...] = halves(state[...])[1]


def state_kernel(
    tot, raw, cum_in, cum_rows, gate, local, incoming, step_bias, skip, hide, spread,
    ssd_o, start_o, squares_o,
    state,
):
    width = gate.shape[1]

    @pl.when(pl.program_id(0) == 0)
    def _():
        state[...] = incoming[...]

    inner = silu(tot[:, :width])
    keys = silu(tot[:, width : width + LANES]).astype(BF16)
    queries = silu(tot[:, width + LANES :])
    _, step = steps(raw[...], padded_row(step_bias[...]))
    cum = cum_in[...]
    start = state[...]
    start_o[0] = start
    state[...] = state_decay(cum[cum.shape[0] - 1 :], spread[...]) * start + local[0]
    scores = dot_left(queries, keys, 1, 1)
    fed = (inner * widen(step, spread[...])).astype(BF16)
    carried = widen(jnp.exp(cum), spread[...]) * dot_both(queries, start, 1, 1)
    head_dim = width // HEADS_OF(width)
    outs = []
    for begin in range(0, width, LANES):
        size = min(LANES, width - begin)
        pair = fed[:, begin : begin + size]
        lane = lax.broadcasted_iota(jnp.int32, (1, size), 1)
        out = None
        for half in range(size // head_dim):
            h = begin // head_dim + half
            decay = jnp.exp(cum[:, h : h + 1] - cum_rows[0, h : h + 1, :] + hide[...])
            part = dot((scores * decay).astype(BF16), pair)
            out = part if out is None else jnp.where(lane < half * head_dim, out, part)
        outs.append(out)
    ssd = jnp.concatenate(outs, 1) + carried + skip_row(skip, spread) * inner
    ssd_o[...] = ssd
    mixed = ssd * silu(gate[...])
    squares_o[0] = as_rows(mixed * mixed)


HEAD_DIM = 64


def HEADS_OF(width):
    return width // HEAD_DIM


def scale_of(squares, width, all_width):
    return lax.rsqrt(as_columns(squares, width) / all_width + eps)


def out_kernel(all_width, ssd, gate, squares, gain, w_out, normed_o, part_o):
    width = ssd.shape[1]
    mixed = ssd[...] * silu(gate[...])
    normed = (mixed * scale_of(squares[0], width, all_width) * gain[...]).astype(BF16)
    normed_o[...] = normed
    for piece in range(w_out.shape[0]):
        part_o[piece] = dot(w_out[piece], normed, 1, 1).astype(BF16)


def cross_kernel(pieces, *refs):
    grads, (w_out, ssd, gate, gain, dn_o, cross_o) = refs[:pieces], refs[pieces:]
    dn = sum(dot(grads[p][...], w_out[p], 0, 0) for p in range(pieces))
    dn_o[...] = dn
    cross_o[0] = as_rows(dn * gain[...] * (ssd[...] * silu(gate[...])))


def gate_kernel(pieces, all_width, *refs):
    grads = refs[:pieces]
    (
        ssd, gate, dn, tot, cum_in, normed, normed_out, squares, cross, gain, spread,
        dssd_o, dgate_o, local_o, payload_o, fine_o, gw_out_o, gw_gate_o, sums_o,
        state, passed,
    ) = refs[pieces:]
    width, length = ssd.shape[1], ssd.shape[0]

    @pl.when(pl.program_id(0) == 0)
    def _():
        state[...] = jnp.zeros_like(state)
        passed[...] = jnp.zeros_like(passed)
        gw_out_o[...] = jnp.zeros_like(gw_out_o)
        gw_gate_o[...] = jnp.zeros_like(gw_gate_o)
        sums_o[...] = jnp.zeros_like(sums_o)

    g = gate[...]
    s = jax.nn.sigmoid(g)
    act = g * s
    mixed = ssd[...] * act
    scale = scale_of(squares[0], width, all_width)
    dscaled = dn[...] * scale
    along = as_columns(cross[0] / (squares[0] + all_width * eps), width)
    dmixed = scale * (dn[...] * gain[...] - mixed * along)
    dssd = dmixed * act
    dssd_o[...] = dssd
    dgate = (dmixed * ssd[...] * s * (1.0 + g * (1.0 - s))).astype(BF16)
    dgate_o[...] = dgate
    inner = silu(tot[:, :width])
    queries = silu(tot[:, width + LANES :])
    sums_o[0:1] = sums_o[0:1] + row_sum(dscaled * mixed)
    sums_o[1:2] = sums_o[1:2] + row_sum(dssd * inner)
    cum = cum_in[...]
    local = dot_both(widen(jnp.exp(cum), spread[...]) * dssd, queries, 0, 0)
    local_o[0] = local
    state[...] = state_decay(cum[length - 1 :], spread[...]) * state[...] + local
    passed[...] = passed[...] + cum[length - 1 :]
    for p in range(pieces):
        gw_out_o[p] = gw_out_o[p] + dot(grads[p][...], normed_out[...])
    gw_gate_o[...] = gw_gate_o[...] + dot(normed[...], dgate, 0, 0)
    write_payload(payload_o, state, passed, fine_o)


def pull_kernel(
    tot, raw, cum_in, cum_rows, dssd, start, local, outgoing, step_bias, decay_log, skip, lower, hide, spread,
    d_o, draw_o, sums_o,
    state,
):
    width, length = dssd.shape[1], dssd.shape[0]

    @pl.when(pl.program_id(0) == 0)
    def _():
        state[...] = outgoing[...]
        sums_o[...] = jnp.zeros_like(sums_o)

    inner = silu(tot[:, :width])
    keys = silu(tot[:, width : width + LANES]).astype(BF16)
    queries = silu(tot[:, width + LANES :])
    shifted_raw, step = steps(raw[...], padded_row(step_bias[...]))
    growth = jnp.exp(padded_row(decay_log[...]))
    rate = -growth * step
    cum = cum_in[...]
    last = cum[length - 1 : length]
    ending = state[...]
    state[...] = state_decay(last, spread[...]) * ending + local[0]
    beginning = start[0]
    dy = dssd[...]
    dy16, dy_fine = halves(dy)
    ecum = jnp.exp(cum)
    tail = jnp.exp(last - cum)
    step_w = widen(step, spread[...])
    ecum_w = widen(ecum, spread[...])
    tail_w = widen(tail * step, spread[...])
    read = dot(queries.astype(BF16), beginning.astype(BF16), 1, 1)
    dqueries = dot_both(ecum_w * dy, beginning)
    taken = dot(keys, ending.astype(BF16), 1, 1)
    dkeys = dot_right((tail_w * inner).astype(BF16), ending)
    from_start = ecum * narrow(dy * read, spread[...])
    to_end = tail * narrow(inner * taken, spread[...])
    both = as_rows(ending * beginning)
    through = jnp.exp(last) * narrow(both, spread[...])[0:1]
    scores = dot_left(queries, keys, 1, 1)
    fed = (inner * step_w).astype(BF16)
    dscores = jnp.zeros_like(scores)
    crossing = jnp.zeros((length, LANES), F32)
    pulls, downs = [], []
    lanes_all = lax.broadcasted_iota(jnp.int32, (length, LANES), 1)
    for begin in range(0, width, LANES):
        size = min(LANES, width - begin)
        fed_pair, dy_pair, dy_low = (v[:, begin : begin + size] for v in (fed, dy16, dy_fine))
        lane = lax.broadcasted_iota(jnp.int32, (1, size), 1)
        rows = []
        for half in range(size // HEAD_DIM):
            h = begin // HEAD_DIM + half
            inside = (lane >= half * HEAD_DIM) & (lane < (half + 1) * HEAD_DIM)
            fed_head = jnp.where(inside, fed_pair, jnp.zeros_like(fed_pair))
            decay = jnp.exp(cum[:, h : h + 1] - cum_rows[0, h : h + 1, :] + hide[...])
            dweight = dot(dy_pair, fed_head, 1, 1) + dot(dy_low, fed_head, 1, 1)
            dweight = dweight * decay
            dscores = dscores + dweight
            weight = (scores * decay).astype(BF16)
            pulled = dot(dy_pair, weight, 0, 0)
            rows.append(pulled[half * HEAD_DIM : (half + 1) * HEAD_DIM])
            pair_terms = dweight * scores
            right = jnp.sum(pair_terms, 1, keepdims=True)
            downs.append(jnp.sum(pair_terms, 0, keepdims=True))
            crossing = jnp.where(lanes_all == h, right, crossing)
        pulls.append(jnp.concatenate(rows, 0).T)
    pulled = jnp.concatenate(pulls, 1)
    downs.append(jnp.zeros((LANES - len(downs), length), F32))
    crossing = crossing - jnp.concatenate(downs, 0).T
    coarse, fine = halves(dscores)
    dqueries = dqueries + dot(coarse, keys) + dot(fine, keys)
    dkeys = dkeys + (dot_left(queries, coarse, 0, 0) + dot(queries.astype(BF16), fine, 0, 0)).T
    dinner = (tail_w * taken + step_w * pulled) + skip_row(skip, spread) * dy
    dstep = narrow(inner * pulled, spread[...]) + to_end
    given = to_end * step
    drate = dot_right(lower[...], crossing + from_start, 0, 0) + (dot_right(lower[...], given) - given)
    drate = drate + through
    dstep = dstep - growth * drate
    draw = dstep * jax.nn.sigmoid(shifted_raw)
    draw_o[...] = draw
    sums_o[0:1] = sums_o[0:1] + row_sum(draw)
    sums_o[1:2] = sums_o[1:2] + row_sum(rate * drate)
    d_o[:, :width] = dinner * silu_slope(tot[:, :width])
    d_o[:, width : width + LANES] = dkeys * silu_slope(tot[:, width : width + LANES])
    d_o[:, width + LANES :] = dqueries * silu_slope(tot[:, width + LANES :])


def project_kernel(
    earlier, d, halo, pre, normed, dgate, draw, gate_sums, rate_sums, taps_a, taps_b, w_gate, w_inner, w_bc, w_step, *refs
):
    given, (part_o, *totals, after) = refs[:earlier], refs[earlier:]
    gw_inner_o, gw_bc_o, sums_o = totals
    width, length = w_gate.shape[1], d.shape[0]

    @pl.when(pl.program_id(0) == 0)
    def _():
        after[...] = halo[...]
        for at, out in enumerate(totals):
            out[...] = given[at][...] if earlier else jnp.zeros_like(out)
        if not earlier:
            rows = jnp.concatenate([gate_sums[0:2], rate_sums[0:2], jnp.zeros((2, LANES), F32)], 1)
            sums_o[taps_a.shape[0] + 1 : taps_a.shape[0] + 3, : rows.shape[1]] = rows

    taps = jnp.concatenate([taps_a[...], taps_b[...]], 1)
    kernel, heads, both = taps.shape[0], w_step.shape[1], taps.shape[1]
    features = normed.shape[1]
    grads = d[...]
    padded = jnp.concatenate([grads, after[...]], 0)
    after[...] = grads[:8]
    dpre = jnp.zeros_like(grads)
    for k in range(kernel):
        moved = padded[kernel - 1 - k : kernel - 1 - k + length]
        dpre = dpre + taps[k : k + 1, :] * moved
        sums_o[k : k + 1, :both] = sums_o[k : k + 1, :both] + row_sum(pre[...] * moved)
    sums_o[kernel : kernel + 1, :both] = sums_o[kernel : kernel + 1, :both] + row_sum(grads)
    dinner, dbc, dstep = dpre[:, :width].astype(BF16), dpre[:, width:], draw[:, :heads].astype(BF16)
    part = dot(dgate[...], w_gate[...], 1, 1) + dot(dinner, w_inner[...], 1, 1)
    part = part + dot_left(dbc, w_bc[...], 1, 1) + dot(dstep, w_step[...], 1, 1)
    part_o[...] = part.astype(BF16)
    gw_inner_o[...] = gw_inner_o[...] + dot(normed[...], dinner, 0, 0)
    gw_bc_o[...] = gw_bc_o[...] + dot_right(normed[...], dbc, 0, 0)
    sums_o[8 : 8 + heads, :features] = sums_o[8 : 8 + heads, :features] + dot(dstep, normed[...], 0, 0)


def input_kernel(place, dnormed, x, gain, *refs):
    pieces = len(refs) - 3
    grads, (block_o, sums_o, columns) = refs[:pieces], refs[pieces:]
    for p in range(pieces):
        columns[(place[0] - p + pieces) % pieces] = grads[p][...].astype(F32)
    cotangent = jnp.concatenate([columns[q] for q in range(pieces)], 0).T
    rows = x[...].astype(F32)
    scale = lax.rsqrt(jnp.mean(rows * rows, -1, keepdims=True) + eps)
    scaled = dnormed[...] * gain[...]
    sums_o[...] = jnp.broadcast_to(row_sum(dnormed[...] * rows * scale), sums_o.shape)
    along = rows * (scale * scale * scale * jnp.mean(scaled * rows, -1, keepdims=True))
    block_o[...] = (scaled * scale - along + cotangent).astype(BF16)


def input_call(mine, side, dnormed, layer_input, gain, cotangents):
    rows, features = dnormed.shape
    pieces = len(cotangents)
    piece = cotangents[0].shape[0]
    return pl.pallas_call(
        input_kernel,
        grid_spec=pltpu.PrefetchScalarGridSpec(
            num_scalar_prefetch=1,
            grid=(1,),
            in_specs=[
                pl.BlockSpec((rows, features), lambda i, place: (0, 0)),
                pl.BlockSpec((rows, features), lambda i, place: (side * pieces + place[0], 0)),
                pl.BlockSpec((1, features), lambda i, place: (0, 0)),
            ]
            + [pl.BlockSpec((piece, rows), lambda i, place: (0, side * pieces + place[0]))] * pieces,
            out_specs=[
                pl.BlockSpec((rows, features), lambda i, place: (0, 0)),
                pl.BlockSpec((8, features), lambda i, place: (0, 0)),
            ],
            scratch_shapes=[pltpu.VMEM((pieces, piece, rows), F32)],
        ),
        out_shape=[jax.ShapeDtypeStruct((rows, features), BF16), jax.ShapeDtypeStruct((8, features), F32)],
        compiler_params=pltpu.CompilerParams(
            dimension_semantics=("arbitrary",), vmem_limit_bytes=60 * 1024 * 1024
        ),
        cost_estimate=pl.CostEstimate(flops=10**6, bytes_accessed=10**4, transcendentals=0),
    )(mine[None].astype(jnp.int32), dnormed, layer_input, gain, *cotangents)


def assemble_kernel(given, place, *refs):
    blocks, out = refs[given:-1], refs[-1]
    wanted = (place[0] - pl.program_id(0) + len(blocks)) % len(blocks)
    for at, block in enumerate(blocks):

        @pl.when(wanted == at)
        def _():
            out[...] = block[...].astype(F32)


def assemble_call(mine, side, blocks, total, given=()):
    rows, features = blocks[0].shape
    pieces = len(blocks)
    return pl.pallas_call(
        functools.partial(assemble_kernel, len(given)),
        grid_spec=pltpu.PrefetchScalarGridSpec(
            num_scalar_prefetch=1,
            grid=(pieces,),
            in_specs=[pl.BlockSpec(memory_space=pl.ANY)] * len(given)
            + [pl.BlockSpec((rows, features), lambda i, place: (0, 0))] * pieces,
            out_specs=pl.BlockSpec((rows, features), lambda i, place: (side * pieces + i, 0)),
        ),
        out_shape=jax.ShapeDtypeStruct((total, features), F32),
        input_output_aliases={1: 0} if given else {},
        compiler_params=pltpu.CompilerParams(
            dimension_semantics=("arbitrary",), vmem_limit_bytes=60 * 1024 * 1024
        ),
        cost_estimate=pl.CostEstimate(flops=10**6, bytes_accessed=10**4, transcendentals=0),
    )(mine[None].astype(jnp.int32), *given, *blocks)


def call(kernel, blocks, ins, outs, scratch=(), backward=False, total=None, skipped=0):
    steps_here = blocks

    def spec(shape, kind, blocks=blocks, skipped=0):
        def at(i):
            return skipped + (steps_here - 1 - i if backward else i)

        if kind == "rows":
            return pl.BlockSpec((shape[0] // blocks,) + shape[1:], lambda i: (at(i), 0))
        if kind == "stack":
            return pl.BlockSpec((1,) + shape[1:], lambda i: (at(i), 0, 0))
        if kind == "columns":
            return pl.BlockSpec((shape[0], shape[1] // blocks), lambda i: (0, at(i)))
        if kind == "last":
            return pl.BlockSpec((shape[0], shape[1], shape[2] // blocks), lambda i: (0, 0, at(i)))
        return pl.BlockSpec(shape, lambda i: (0,) * len(shape))

    return pl.pallas_call(
        kernel,
        grid=(blocks,),
        in_specs=[spec(a.shape, kind, total or blocks, skipped) for a, kind in ins],
        out_specs=[spec(shape, kind) for shape, _, kind in outs],
        out_shape=[jax.ShapeDtypeStruct(shape, dtype) for shape, dtype, _ in outs],
        scratch_shapes=[pltpu.VMEM(shape, F32) for shape in scratch],
        compiler_params=pltpu.CompilerParams(
            dimension_semantics=("arbitrary",), vmem_limit_bytes=60 * 1024 * 1024
        ),
        cost_estimate=pl.CostEstimate(flops=10**6, bytes_accessed=10**4, transcendentals=0),
    )(*[a for a, _ in ins])


def per_device(
    layer_input, gain_in, w_gate, w_inner, w_bc, w_step, conv_inner, conv_inner_bias, conv_bc, conv_bc_bias,
    step_bias, decay_log, skip_gain, gain_out, w_out, output_grad,
):
    count, features = layer_input.shape
    heads, width = decay_log.shape[0], w_gate.shape[1]
    states = w_bc.shape[1] // 2
    both = width + 2 * states
    blocks = count // BLOCK
    kernel = conv_inner.shape[0]
    pieces, mine = lax.axis_size("head"), lax.axis_index("head")
    all_width = width * pieces
    piece = output_grad.shape[1]
    rows = count // pieces

    place = np.arange(BLOCK)
    keep = place[:, None] >= place[None, :]
    lower = jnp.asarray(keep, BF16)
    hide = jnp.asarray(np.where(keep, 0.0, -1e30), F32)
    spread = jnp.asarray(np.arange(LANES)[:, None] == (np.arange(width) // (width // heads))[None, :], BF16)
    bias_row, decay_row, skip = step_bias[None], decay_log[None], skip_gain[None]
    gain_out_row = gain_out[None]
    w_out_pieces = w_out.T.reshape(pieces, piece, width)
    owners = (mine - jnp.arange(pieces)) % pieces
    w_out_ring = jnp.take(w_out_pieces, owners, axis=0)

    halo = shifted(layer_input[count - EDGE :], "seq", 1)
    halo, grad_columns = tie(halo, output_grad.T)
    cotangents = [grad_columns, turn(grad_columns, "head", 1)]

    whole = lambda *arrays: [(a, "whole") for a in arrays]
    normed, gate, pre, tot, raw, cum, cum_rows, local, payload, fine = call(
        forward_kernel,
        blocks,
        [(layer_input, "rows")]
        + whole(halo, gain_in[None], w_gate, w_inner, w_bc, w_step, conv_inner, conv_bc)
        + whole(conv_inner_bias[None], conv_bc_bias[None], bias_row, decay_row, lower, spread),
        [
            ((count, features), BF16, "rows"),
            ((count, width), F32, "rows"),
            ((count, both), F32, "rows"),
            ((count, both), F32, "rows"),
            ((count, LANES), F32, "rows"),
            ((count, LANES), F32, "rows"),
            ((blocks, 8, BLOCK), F32, "stack"),
            ((blocks, width, states), F32, "stack"),
            ((width + 16, states), BF16, "whole"),
            ((width, states), BF16, "whole"),
        ],
        [(8, both), (width, states), (16, LANES)],
    )
    payload, cotangents[1] = tie(payload, cotangents[1])
    cotangents.append(turn(cotangents[1], "head", 1))
    gathered = lax.all_gather(payload, "seq")
    gathered, fine, cotangents[2] = tie(gathered, fine, cotangents[2])
    incoming = joined_states(gathered, "seq", width, heads, False, lax.all_gather(fine, "seq"))
    for _ in range(pieces - 3):
        cotangents.append(turn(cotangents[-1], "head", 1))
    ssd, starts, squares = call(
        state_kernel,
        blocks,
        [(tot, "rows"), (raw, "rows"), (cum, "rows"), (cum_rows, "stack"), (gate, "rows"), (local, "stack")]
        + whole(incoming, bias_row, skip, hide, spread),
        [
            ((count, width), F32, "rows"),
            ((blocks, width, states), F32, "stack"),
            ((blocks, 8, BLOCK), F32, "stack"),
        ],
        [(width, states)],
    )
    squares, cotangents[-1] = tie(squares, cotangents[-1])
    squares = small_sum(squares, "head")
    dn, cross = call(
        functools.partial(cross_kernel, pieces),
        blocks,
        [(c, "columns") for c in cotangents]
        + whole(w_out_ring)
        + [(ssd, "rows"), (gate, "rows")]
        + whole(gain_out_row),
        [((count, width), F32, "rows"), ((blocks, 8, BLOCK), F32, "stack")],
    )
    cross = small_sum(cross, "head")
    squares_out, dn = tie(squares, dn)
    normed_out, mixed_parts = call(
        functools.partial(out_kernel, all_width),
        blocks,
        [(ssd, "rows"), (gate, "rows"), (squares_out, "stack")] + whole(gain_out_row, w_out_pieces),
        [((count, width), BF16, "rows"), ((pieces, piece, count), BF16, "last")],
    )
    mixed_parts, cross = tie(mixed_parts, cross)
    mixed_ring = ring_scatter(lambda q: lax.dynamic_index_in_dim(mixed_parts, q, 0, False), "head")
    arrived = next(mixed_ring)

    dssd, dgate, local_back, payload_back, fine_back, gw_out, gw_gate, gate_sums = call(
        functools.partial(gate_kernel, pieces, all_width),
        blocks,
        [(c, "columns") for c in cotangents]
        + [(a, "rows") for a in (ssd, gate, dn, tot, cum, normed, normed_out)]
        + [(squares, "stack"), (cross, "stack")]
        + whole(gain_out_row, spread),
        [
            ((count, width), F32, "rows"),
            ((count, width), BF16, "rows"),
            ((blocks, width, states), F32, "stack"),
            ((width + 16, states), BF16, "whole"),
            ((width, states), BF16, "whole"),
            ((pieces, piece, width), F32, "whole"),
            ((features, width), F32, "whole"),
            ((8, width), F32, "whole"),
        ],
        [(width, states), (16, LANES)],
        backward=True,
    )
    payload_back, arrived = tie(payload_back, arrived)
    gathered_back = lax.all_gather(payload_back, "seq")
    for _ in range(pieces - 3):
        arrived = mixed_ring.send(arrived)
    outgoing = joined_states(gathered_back, "seq", width, heads, True, lax.all_gather(fine_back, "seq"))
    d, draw, rate_sums = call(
        pull_kernel,
        blocks,
        [(tot, "rows"), (raw, "rows"), (cum, "rows"), (cum_rows, "stack"), (dssd, "rows"), (starts, "stack"), (local_back, "stack")]
        + whole(outgoing, bias_row, decay_row, skip, lower, hide, spread),
        [((count, both), F32, "rows"), ((count, LANES), F32, "rows"), ((8, LANES), F32, "whole")],
        [(width, states)],
        backward=True,
    )
    d, arrived = tie(d, arrived)
    arrived = mixed_ring.send(arrived)

    half, half_rows = count // 2, rows // 2
    halo_d = shifted(d[:8], "seq", -1)
    shares, totals = [None, None], []
    for side in (1, 0):
        part, *totals = call(
            functools.partial(project_kernel, len(totals)),
            blocks // 2,
            [(d, "rows")]
            + whole(halo_d)
            + [(pre, "rows"), (normed, "rows"), (dgate, "rows"), (draw, "rows")]
            + whole(gate_sums, rate_sums, conv_inner, conv_bc, w_gate, w_inner, w_bc, w_step, *totals),
            [
                ((half, features), BF16, "rows"),
                ((features, width), F32, "whole"),
                ((features, 2 * states), F32, "whole"),
                ((16, max(features, both)), F32, "whole"),
            ],
            [(8, both)],
            backward=True,
            total=blocks,
            skipped=side * (blocks // 2),
        )
        halo_d = d[half : half + 8]
        if side:
            d, arrived, gw_out, gw_gate = tie(d, arrived, *lax.psum((gw_out, gw_gate), "seq"))
        shares[side] = ring_scatter(
            lambda q, part=part: lax.dynamic_slice_in_dim(part, q * half_rows, half_rows, 0), "head"
        )
        running = next(shares[side])
        if side:
            first = running
        else:
            first, part = tie(first, part)
    gw_inner, gw_bc, conv_sums = totals

    gain_row = gain_in[None]
    runs, blocks_of, sums = {1: first, 0: running}, {}, {}
    runs[1], gw_inner, gw_bc, conv_sums = tie(runs[1], gw_inner, gw_bc, conv_sums)
    chores = Chores(weight_chores(gw_inner, gw_bc, conv_sums, width))
    for step in range(pieces - 1):
        for side in (1, 0):
            runs[side] = shares[side].send(runs[side])
            if side and step < pieces - 2:
                runs[1] = chores.beside(runs[1])
    runs[0], arrived, layer_late = tie(runs[0], arrived, layer_input)
    for side in (1, 0):
        blocks_of[side], sums[side] = input_call(mine, side, runs[side], layer_input, gain_row, cotangents)
    summed = mixed_ring.send(arrived)
    residual = lax.dynamic_slice_in_dim(layer_late, mine * piece, piece, 1).astype(F32)
    mixed = (residual.T + summed).astype(BF16).T

    arrivals = {side: [blocks_of[side]] for side in (0, 1)}
    for step in range(1, pieces):
        for side in (1, 0):
            blocks_of[side] = turn(blocks_of[side], "head", 1)
            if step > 1 or side:
                blocks_of[side] = chores.beside(blocks_of[side])
            if step == 1 and side:
                blocks_of[1], gain_part = tie(blocks_of[1], (sums[0] + sums[1])[0].reshape(-1, LANES))
                gains = Chores(gain_chores((gain_part,)))
            elif step > 1:
                blocks_of[side] = gains.beside(blocks_of[side])
            arrivals[side].append(blocks_of[side])
            if step == 1 and not side:
                blocks_of[0], gw_out = tie(blocks_of[0], gw_out)
    grad_input = assemble_call(mine, 1, arrivals[1], count)
    grad_input = assemble_call(mine, 0, arrivals[0], count, (grad_input,))
    gw_inner, gw_bc, sums, bc_sums = chores.finish()
    grad_gain_in = gains.finish()[0].reshape(-1)
    gw_out = jnp.take(gw_out, owners, axis=0).reshape(features, width).T
    head_dim = width // heads
    return (
        mixed,
        grad_input,
        grad_gain_in,
        gw_gate,
        gw_inner,
        gw_bc,
        sums[8 : 8 + heads, :features].T,
        sums[:kernel, :width],
        sums[kernel, :width],
        bc_sums[:kernel],
        bc_sums[kernel],
        sums[kernel + 1, width : width + heads],
        sums[kernel + 2, width : width + heads],
        sums[kernel + 2, :width].reshape(heads, head_dim).sum(1),
        sums[kernel + 1, :width],
        gw_out,
    )


def solution(mesh):
    placed = (
        P("seq", None),
        P(),
        P(None, "head"),
        P(None, "head"),
        P(),
        P(None, "head"),
        P(None, "head"),
        P("head"),
        P(),
        P(),
        P("head"),
        P("head"),
        P("head"),
        P("head"),
        P("head", None),
        P("seq", "head"),
    )
    return jax.shard_map(
        per_device,
        mesh=mesh,
        in_specs=placed,
        out_specs=(
            P("seq", "head"),
            P("seq", None),
            P(),
            P(None, "head"),
            P(None, "head"),
            P(),
            P(None, "head"),
            P(None, "head"),
            P("head"),
            P(),
            P(),
            P("head"),
            P("head"),
            P("head"),
            P("head"),
            P("head", None),
        ),
        check_vma=False,
    )
```
